512 devices in a mesh: tm: 64 (over x, z_lo, y), rows: 8 (over z_hi, core).
Axes of the slice: x: 4, y: 8, z: 8 (z_hi: 4, z_lo: 2; z = z_hi * 2 + z_lo), core: 2. Of those that a mesh axis runs over, the one named last changes fastest.
Arguments:
- activations: bfloat16 [256, 16, 32, 256], P('tm', 'rows'), may hold values from -6 to 6
- cotangent: bfloat16 [256, 16, 32, 256], P('tm', 'rows'), may hold values from -6 to 6
- gain: float32 [256], replicated, may hold values from 0.1 to 1.9
- first_weight: bfloat16 [6912, 256], P('tm'), may hold values from -0.078125 to 0.078125
- second_weight: bfloat16 [6912, 256], P('tm'), may hold values from -0.078125 to 0.078125
Outputs:
- input_grad: bfloat16 [256, 16, 32, 256], P('tm', 'rows')
- weight_grad: float32 [6912, 128], P('tm')
The draws below stay inside these ranges and needn't reach their ends.
All inputs are finite; a program needn't handle non-finite values.
Results may differ from the reference program's by a relative error of at most 0.017.
Values may be sent and summed in bfloat16 or wider, within the bound.
No kernel may reach another device: no remote copies, remote signals or barrier semaphores. Data moves between devices by JAX's collectives and lax.ppermute only.
A program may use at most 64 MiB of HBM per device.

```python
import jax
import jax.numpy as jnp
from jax import lax

C = 256
CH = 128
W = 32
FRAMES = 256
H = 16


def level_of(key, extent, shards, smallest, largest):
    level, own = 1.0, jax.random.fold_in(key, 6)
    for axis_at, blocks in shards:
        heights = jnp.exp(jax.random.uniform(jax.random.fold_in(own, axis_at), (blocks,), jnp.float32, smallest / len(shards), largest / len(shards)))
        level = level * jnp.repeat(heights, extent[axis_at] // blocks).reshape([-1 if axis == axis_at else 1 for axis in range(len(extent))])
    return level


def scatter_about(rng, dims, spread, limit, pieces=(), held_as=jnp.bfloat16):
    entries = jax.random.normal(rng, dims, jnp.float32) * spread
    if len(pieces) > 0:
        entries = level_of(rng, dims, pieces, -0.22, 0.18) * entries
    return jnp.clip(entries, min=-limit, max=limit).astype(held_as)


def setup_inputs(seed: int = 0) -> dict:
    streams_of = jax.random.split(jax.random.key(seed), 6)
    activations = scatter_about(streams_of[0], (FRAMES, H, W, C), 1.0, 6.0, ((0, 64), (1, 8)))
    cotangent = scatter_about(streams_of[1], (FRAMES, H, W, C), 1.0, 6.0, ((0, 64), (1, 8)))
    gain = jnp.clip(1.0 + 0.18 * jax.random.normal(streams_of[2], (C,), jnp.float32), 0.1, 1.9)
    first_weight = scatter_about(streams_of[3], (27 * C, C), (27 * C) ** -0.5, 0.078125, ((0, 64),))
    second_weight = scatter_about(streams_of[4], (27 * C, C), (27 * C) ** -0.5, 0.078125, ((0, 64),))
    return dict(activations=activations, cotangent=cotangent, gain=gain, first_weight=first_weight, second_weight=second_weight)


epsilon = 1e-06

def tap_list():
    return [(along_t, along_h, along_w) for along_t in range(3) for along_h in range(3) for along_w in range(3)]

def forward_conv(padded, weight, frames, row_count, col_count):
    channels = padded.shape[3]
    total = jnp.zeros((frames * row_count * col_count, weight.shape[1]), jnp.float32)
    for number, (along_t, along_h, along_w) in enumerate(tap_list()):
        piece = padded[along_t:along_t + frames, along_h:along_h + row_count, along_w:along_w + col_count].reshape(-1, channels)
        total = total + jnp.dot(piece, weight[number * channels:(number + 1) * channels], preferred_element_type=jnp.float32)
    return total

def transpose_conv(padded, weight, frames, row_count, col_count):
    channels = padded.shape[3]
    total = jnp.zeros((frames * row_count * col_count, channels), jnp.float32)
    for number, (along_t, along_h, along_w) in enumerate(tap_list()):
        piece = padded[2 - along_t:2 - along_t + frames, 2 - along_h:2 - along_h + row_count, 2 - along_w:2 - along_w + col_count].reshape(-1, channels)
        block = weight[number * channels:(number + 1) * channels]
        total = total + jnp.dot(piece, block.T, preferred_element_type=jnp.float32)
    return total

def reference(activations, cotangent, gain, first_weight, second_weight):
    frames, row_count, col_count, channels = activations.shape
    x_pad = jnp.pad(activations, ((2, 0), (1, 1), (1, 1), (0, 0)))
    pre = forward_conv(x_pad, first_weight, frames, row_count, col_count)
    scale = lax.rsqrt(lax.optimization_barrier(jnp.mean(pre * pre, axis=-1, keepdims=True)) + epsilon)
    normed = pre * scale
    gated = normed * gain
    sigma = jax.nn.sigmoid(gated)
    act = (gated * sigma).astype(jnp.bfloat16).reshape(frames, row_count, col_count, channels)
    dy_pad = jnp.pad(cotangent, ((0, 2), (1, 1), (1, 1), (0, 0)))
    act_grad = transpose_conv(dy_pad, second_weight, frames, row_count, col_count)
    norm_grad = act_grad * sigma * (1.0 + gated * (1.0 - sigma)) * gain
    pre_grad = scale * (norm_grad - normed * lax.optimization_barrier(jnp.mean(norm_grad * normed, axis=-1, keepdims=True)))
    pre_grad = pre_grad.astype(jnp.bfloat16).reshape(frames, row_count, col_count, channels)
    dh_pad = jnp.pad(pre_grad, ((0, 2), (1, 1), (1, 1), (0, 0)))
    input_grad = transpose_conv(dh_pad, first_weight, frames, row_count, col_count)
    input_grad = input_grad.astype(jnp.bfloat16).reshape(frames, row_count, col_count, channels)
    a_pad = jnp.pad(act, ((2, 0), (1, 1), (1, 1), (0, 0)))
    dy_cols = cotangent.reshape(-1, channels)[:, :CH]
    blocks = []
    for along_t, along_h, along_w in tap_list():
        piece = a_pad[along_t:along_t + frames, along_h:along_h + row_count, along_w:along_w + col_count].reshape(-1, channels)
        blocks.append(jnp.dot(piece.T, dy_cols, preferred_element_type=jnp.float32))
    weight_grad = jnp.concatenate(blocks, axis=0)
    return (input_grad, weight_grad)
```

```python
import functools

import jax
import jax.numpy as jnp
from jax import lax
from jax.experimental import pallas as pl
from jax.experimental.pallas import tpu as pltpu
from jax.sharding import PartitionSpec as P

CH = 128
C = 256
W = 32
HALF = 128
ROWS = 6912
EPS = 1e-06
BF = jnp.bfloat16
F32 = jnp.float32

YZ_GROUPS = [[x * 16 + k for k in range(16)] for x in range(4)]
X_GROUPS = [[x * 16 + k for x in range(4)] for k in range(16)]
Y_GROUPS = [[b * 8 + k for k in range(8)] for b in range(8)]
CORE_GROUPS = [[2 * z, 2 * z + 1] for z in range(4)]


def spread(block, axis, groups):
    count = len(groups[0])
    operand = jnp.broadcast_to(block[None], (count,) + block.shape)
    return lax.all_to_all(operand, axis, 0, 0, axis_index_groups=groups, tiled=True)


def swap(block, axis, mask):
    count = lax.axis_size(axis)
    return lax.ppermute(block, axis, [(i, i ^ mask) for i in range(count)])


def in_order(blocks, low, high):
    a, b, c, d = blocks
    a, b = jnp.where(low, b, a), jnp.where(low, a, b)
    c, d = jnp.where(low, d, c), jnp.where(low, c, d)
    a, c = jnp.where(high, c, a), jnp.where(high, a, c)
    b, d = jnp.where(high, d, b), jnp.where(high, b, d)
    return jnp.stack([a, b, c, d])


def exchange(block, index, low_mask, high_mask):
    blocks = [block] + [swap(block, "tm", m) for m in (low_mask, high_mask, low_mask | high_mask)]
    return in_order(blocks, (index & low_mask) != 0, (index & high_mask) != 0)


def shift_ppermute(block, axis, distance):
    count = lax.axis_size(axis)
    route = [(i, i + distance) for i in range(count) if 0 <= i + distance < count]
    return lax.ppermute(block, axis, route)


def fill_shifts(out, piece, at, column_of):
    frames, rows = piece.shape[:2]
    flat = piece.reshape(frames * rows * W, piece.shape[3]).astype(F32)
    column = column_of(flat.shape)
    before = jnp.where(column == 0, 0.0, pltpu.roll(flat, 1, 0))
    after = jnp.where(column == W - 1, 0.0, pltpu.roll(flat, flat.shape[0] - 1, 0))
    out[1, :, at : at + rows] = piece
    out[0, :, at : at + rows] = before.astype(BF).reshape(piece.shape)
    out[2, :, at : at + rows] = after.astype(BF).reshape(piece.shape)


def column_of(shape):
    return lax.broadcasted_iota(jnp.int32, shape, 0) % W


def normalize(pre, gain):
    scale = lax.rsqrt(jnp.mean(pre * pre, axis=-1, keepdims=True) + EPS)
    normed = pre * scale
    gated = normed * gain
    sigma = 1.0 / (1.0 + jnp.exp(-gated))
    return scale, normed, gated, sigma


def forward_kernel(x_lo, x_mid, x_hi, g_lo, g_mid, g_hi, gain, w1, pre_ref, wg_ref, xs, cs):
    for n, piece in enumerate((x_lo, x_mid, x_hi)):
        for f in range(0, 8, 2):
            fill_shifts(xs.at[:, f : f + 2], piece[f : f + 2], 2 * n, column_of)
    for n, piece in enumerate((g_lo, g_mid, g_hi)):
        for f in range(0, 6, 2):
            fill_shifts(cs.at[:, f : f + 2], piece[f : f + 2, :, :, :CH], 2 * n, column_of)
    for i in range(3):
        for j in range(3):
            lhs = jnp.concatenate(
                [xs[k, i : i + 6, j : j + 4].reshape(768, C) for k in range(3)], axis=1
            )
            at = (i * 3 + j) * 3 * C
            rhs = jnp.concatenate([w1[0, at : at + 3 * C], w1[1, at : at + 3 * C]], axis=1)
            part = jnp.dot(lhs, rhs, preferred_element_type=F32).reshape(6, 4, W, C)
            if i == 0 and j == 0:
                pre_ref[...] = part
            else:
                pre_ref[...] += part
    _, _, gated, sigma = normalize(pre_ref[:4, 1:3].reshape(256, C), gain[...])
    act_t = (gated * sigma).T.astype(BF)
    for i in range(3):
        for j in range(3):
            for k in range(3):
                rhs = cs[2 - k, 2 - i : 6 - i, 3 - j : 5 - j].reshape(256, CH)
                term = jnp.dot(act_t, rhs, preferred_element_type=F32).astype(BF)
                start = ((i * 3 + j) * 3 + k) * C
                done = 0
                while done < C:
                    block, row = divmod(start + done, 864)
                    count = min(C - done, 864 - row)
                    wg_ref[block % 2, block // 2, row : row + count] = term[done : done + count]
                    done += count


def backward_kernel(flags, g_lo, g_mid, g_hi, gain, pre, w1, w2_own, w2_other, out, cs, ps, acc):
    core_one = flags[2] == 1
    for n, piece in enumerate((g_lo, g_mid, g_hi)):
        for f in range(0, 8, 2):
            here = piece[f : f + 2]
            turned = jnp.concatenate([here[..., HALF:], here[..., :HALF]], axis=-1)
            here = jnp.where(core_one, turned, here)
            fill_shifts(cs.at[:, f : f + 2], here, 2 * n, column_of)
    nt = (((1,), (1,)), ((), ()))
    for i in range(3):
        for j in range(3):
            for k in range(3):
                lhs = cs[2 - k, 2 - i : 8 - i, 2 - j : 6 - j].reshape(768, C)
                at = ((i * 3 + j) * 3 + k) * C
                rhs = jnp.concatenate([w2_own[at : at + C], w2_other[at : at + C]], axis=1)
                part = lax.dot_general(lhs, rhs, nt, preferred_element_type=F32)
                if i == 0 and j == 0 and k == 0:
                    acc[...] = part
                else:
                    acc[...] += part
    for t in range(6):
        for h in range(4):
            at = (t * 4 + h) * W
            scale, normed, gated, sigma = normalize(pre[t, h], gain[...])
            norm_grad = acc[at : at + W] * sigma * (1.0 + gated * (1.0 - sigma)) * gain[...]
            pre_grad = scale * (
                norm_grad - normed * jnp.mean(norm_grad * normed, axis=-1, keepdims=True)
            )
            if t >= 4:
                pre_grad = jnp.where(flags[0] == flags[3], 0.0, pre_grad)
            if h == 0:
                pre_grad = jnp.where(flags[1] == 0, 0.0, pre_grad)
            if h == 3:
                pre_grad = jnp.where(flags[1] == flags[4], 0.0, pre_grad)
            fill_shifts(
                ps.at[:, t : t + 1], pre_grad.astype(BF).reshape(1, 1, W, C), h, column_of
            )
    total = None
    for i in range(3):
        for j in range(3):
            for k in range(3):
                lhs = ps[2 - k, 2 - i : 6 - i, 2 - j : 4 - j].reshape(256, C)
                at = ((i * 3 + j) * 3 + k) * C
                rhs = jnp.concatenate([w1[0, at : at + C], w1[1, at : at + C]], axis=1)
                part = lax.dot_general(lhs, rhs, nt, preferred_element_type=F32)
                if i == 0 and j == 0 and k == 0:
                    acc[:256] = part
                else:
                    acc[:256] += part
    out[...] = acc[:256].reshape(4, 2, W, C).astype(BF)


VMEM = pl.BlockSpec(memory_space=pltpu.VMEM)
SMEM = pl.BlockSpec(memory_space=pltpu.SMEM)
PARAMS = pltpu.CompilerParams(vmem_limit_bytes=48 * 1024 * 1024)


def call_forward(x_parts, g_parts, gain, w1):
    return pl.pallas_call(
        forward_kernel,
        out_shape=(
            jax.ShapeDtypeStruct((6, 4, W, C), F32),
            jax.ShapeDtypeStruct((2, 4, 864, CH), BF),
        ),
        in_specs=[VMEM] * 8,
        out_specs=(VMEM, VMEM),
        scratch_shapes=[pltpu.VMEM((3, 8, 6, W, C), BF), pltpu.VMEM((3, 6, 6, W, CH), BF)],
        compiler_params=PARAMS,
        cost_estimate=pl.CostEstimate(
            flops=2 * 768 * ROWS * C + 2 * 256 * ROWS * CH, bytes_accessed=8 << 20, transcendentals=0
        ),
        name="forward_and_terms",
    )(*x_parts, *g_parts, gain, w1)


def call_backward(flags, g_parts, gain, pre, w1, w2_own, w2_other):
    return pl.pallas_call(
        backward_kernel,
        out_shape=jax.ShapeDtypeStruct((4, 2, W, C), BF),
        in_specs=[SMEM] + [VMEM] * 8,
        out_specs=VMEM,
        scratch_shapes=[
            pltpu.VMEM((3, 8, 6, W, C), BF),
            pltpu.VMEM((3, 6, 4, W, C), BF),
            pltpu.VMEM((768, C), F32),
        ],
        compiler_params=PARAMS,
        cost_estimate=pl.CostEstimate(
            flops=2 * 1024 * ROWS * C, bytes_accessed=10 << 20, transcendentals=0
        ),
        name="input_gradient",
    )(flags, *g_parts, gain, pre, w1, w2_own, w2_other)


def on_device(activations, cotangent, gain, first_weight, second_weight):
    tm, rows = lax.axis_index("tm"), lax.axis_index("rows")
    tm_count, rows_count = lax.axis_size("tm"), lax.axis_size("rows")
    core = rows % 2
    z_lo = (tm // 8) % 2
    gain = gain.reshape(1, C)

    half1 = lax.dynamic_slice_in_dim(first_weight, core * HALF, HALF, axis=1)
    half2 = lax.dynamic_slice_in_dim(second_weight, core * HALF, HALF, axis=1)

    w1 = spread(half1, "tm", YZ_GROUPS).reshape(16 * 108, HALF)
    w1 = spread(w1, "tm", X_GROUPS).reshape(ROWS, HALF)
    w1 = spread(w1, "rows", CORE_GROUPS)

    x_t = jnp.concatenate(
        [
            shift_ppermute(activations[2:], "tm", 1),
            activations,
            shift_ppermute(activations[:2], "tm", -1),
        ],
        axis=0,
    )
    x_parts = (shift_ppermute(x_t, "rows", 1), x_t, shift_ppermute(x_t, "rows", -1))
    g_t = jnp.concatenate([cotangent, shift_ppermute(cotangent, "tm", -1)], axis=0)
    g_parts = (shift_ppermute(g_t, "rows", 1), g_t, shift_ppermute(g_t, "rows", -1))

    w2 = exchange(half2, tm, 2, 4)
    w2 = exchange(w2, tm, 1, 8)
    w2 = w2.reshape(2, 2, 4, 108, HALF).transpose(0, 2, 1, 3, 4).reshape(16 * 108, HALF)
    w2 = exchange(w2, tm, 16, 32).reshape(ROWS, HALF)
    w2_other = swap(w2, "rows", 1)

    pre, terms = call_forward(x_parts, g_parts, gain, w1)

    terms = lax.all_to_all(terms, "rows", 0, 0, axis_index_groups=CORE_GROUPS, tiled=True)
    terms = terms.astype(F32).sum(0).astype(BF)
    terms = lax.all_to_all(terms, "tm", 0, 0, axis_index_groups=X_GROUPS, tiled=True)
    terms = terms.astype(F32).sum(0).astype(BF).reshape(8, 108, CH)
    terms = lax.all_to_all(terms, "tm", 0, 0, axis_index_groups=Y_GROUPS, tiled=True)
    total = terms.astype(F32).sum(0)
    total = total + swap(total, "tm", 8)
    left, right, far = (
        lax.ppermute(total, "rows", [(i, (i + d) % rows_count) for i in range(rows_count)])
        for d in (2, rows_count - 2, 4)
    )
    total = (total + far) + (left + right)
    weight_grad = jnp.where(core == z_lo, total, swap(total, "rows", 1))

    flags = jnp.stack([tm, rows, core, tm_count - 1, rows_count - 1]).astype(jnp.int32)
    input_grad = call_backward(flags, g_parts, gain, pre, w1, w2, w2_other)
    return (input_grad, weight_grad)


def solution(mesh):
    return jax.shard_map(
        on_device,
        mesh=mesh,
        in_specs=(
            P("tm", "rows", None, None),
            P("tm", "rows", None, None),
            P(),
            P("tm", None),
            P("tm", None),
        ),
        out_specs=(P("tm", "rows", None, None), P("tm", None)),
        check_vma=False,
    )
```

```python
import jax
import jax.numpy as jnp
from jax import lax
from jax.experimental import pallas as pl
from jax.experimental.pallas import tpu as pltpu
from jax.sharding import PartitionSpec as P

CH = 128
C = 256
W = 32
HALF = 128
ROWS = 6912
EPS = 1e-06
BF = jnp.bfloat16
F32 = jnp.float32

YZ_GROUPS = [[x * 16 + k for k in range(16)] for x in range(4)]
X_GROUPS = [[k, k + 16, k + 32, k + 48] for k in range(16)]
Z_GROUPS = [[c, c + 2, c + 4, c + 6] for c in range(2)]


def spread(block, axis, groups):
    count = len(groups[0])
    operand = jnp.broadcast_to(block[None], (count,) + block.shape)
    return lax.all_to_all(operand, axis, 0, 0, axis_index_groups=groups, tiled=True)


def swap_cores(block):
    return lax.ppermute(block, "rows", [(i, i ^ 1) for i in range(lax.axis_size("rows"))])


def shift(block, axis, distance):
    count = lax.axis_size(axis)
    route = [(i, i + distance) for i in range(count) if 0 <= i + distance < count]
    return lax.ppermute(block, axis, route)


def from_x(block, mask):
    return lax.ppermute(block, "tm", [(i, i ^ (mask * 16)) for i in range(lax.axis_size("tm"))])


def in_order(blocks, low, high):
    a, b, c, d = blocks
    a, b = jnp.where(low, b, a), jnp.where(low, a, b)
    c, d = jnp.where(low, d, c), jnp.where(low, c, d)
    a, c = jnp.where(high, c, a), jnp.where(high, a, c)
    b, d = jnp.where(high, d, b), jnp.where(high, b, d)
    return jnp.stack([a, b, c, d])


def beyond_chip(block):
    count = lax.axis_size("rows")
    route = [(i - 1, i) for i in range(2, count, 2)] + [(i + 1, i) for i in range(1, count - 1, 2)]
    return lax.ppermute(block, "rows", route)


def after(value, *others):
    return lax.optimization_barrier((value,) + others)[0]


def fill_shifts(out, piece, frames, at):
    count, rows = piece.shape[:2]
    flat = piece.reshape(count * rows * W, piece.shape[3]).astype(F32)
    column = lax.broadcasted_iota(jnp.int32, flat.shape, 0) % W
    before = jnp.where(column == 0, 0.0, pltpu.roll(flat, 1, 0))
    behind = jnp.where(column == W - 1, 0.0, pltpu.roll(flat, flat.shape[0] - 1, 0))
    out[1, frames, pl.ds(at, rows)] = piece
    out[0, frames, pl.ds(at, rows)] = before.astype(BF).reshape(piece.shape)
    out[2, frames, pl.ds(at, rows)] = behind.astype(BF).reshape(piece.shape)


def normalize(pre, squares, gain):
    scale = lax.rsqrt(squares * (1.0 / C) + EPS)
    normed = pre * scale
    gated = normed * gain
    sigma = 1.0 / (1.0 + jnp.exp(-gated))
    return scale, normed, gated, sigma


def shifts_kernel(flags, mid, edge, other, xs, cs):
    core = flags[2]
    for out, base in ((xs, 0), (cs, 8)):
        for f in range(0, 8, 2):
            frames = slice(f, f + 2)
            source = slice(base + f, base + f + 2)
            fill_shifts(out, mid[source], frames, 3)
            fill_shifts(out, edge[source], frames, 1 + 4 * core)
            fill_shifts(out, other[source, :2], frames, 5 - 4 * core)
            fill_shifts(out, other[source, 2:], frames, 0)
            for k in range(3):
                out[k, frames, 7:8] = out[k, frames, 0:1]


def half_kernel(flags, xs, w1, pre, squares):
    base = 2 - 2 * flags[2]
    for i in range(3):
        for j in range(3):
            lhs = jnp.concatenate(
                [xs[k, i : i + 4, pl.ds(base + j, 4)].reshape(512, C) for k in range(3)], axis=1
            )
            at = (i * 3 + j) * 3 * C
            part = jnp.dot(lhs, w1[at : at + 3 * C], preferred_element_type=F32)
            if i == 0 and j == 0:
                pre[...] = part
            else:
                pre[...] += part
    total = jnp.sum(pre[...] * pre[...], axis=1, keepdims=True)
    squares[...] = jnp.broadcast_to(total, (512, HALF))


def terms_kernel(flags, pre, own, other, gain, cs, out):
    base = 2 - 2 * flags[2]
    _, _, gated, sigma = normalize(pre[...], own[...] + other[...], gain[...])
    act = (gated * sigma).T.astype(BF)
    taps = [(i, j, k) for i in range(3) for j in range(3) for k in range(3)]

    def operand(i, j, k):
        return cs[2 - k, 2 - i : 6 - i, pl.ds(base + 2 - j, 4), :, :CH].reshape(512, CH)

    for n in range(0, 27, 2):
        pair = taps[n : n + 2]
        rhs = jnp.concatenate([operand(*tap) for tap in pair], axis=1)
        term = jnp.dot(act, rhs, preferred_element_type=F32).astype(BF)
        for m in range(len(pair)):
            out[(n + m) * HALF : (n + m + 1) * HALF] = term[:, m * CH : (m + 1) * CH]


def halves_in_order(flags, value):
    turned = jnp.concatenate([value[..., HALF:], value[..., :HALF]], axis=-1)
    return jnp.where(flags[2] == 1, turned, value)


def pre_kernel(flags, xs, own, other, pre, acc):
    for i in range(3):
        for j in range(3):
            lhs = jnp.concatenate(
                [xs[k, i : i + 6, j + 1 : j + 5].reshape(768, C) for k in range(3)], axis=1
            )
            at = (i * 3 + j) * 3 * C
            rhs = jnp.concatenate([own[at : at + 3 * C], other[at : at + 3 * C]], axis=1)
            part = jnp.dot(lhs, rhs, preferred_element_type=F32)
            if i == 0 and j == 0:
                acc[...] = part
            else:
                acc[...] += part
    pre[...] = halves_in_order(flags, acc[...])


def backward_kernel(flags, cs, gain, pre, w1_own, w1_other, w2_own, w2_other, out, ps, acc):
    nt = (((1,), (1,)), ((), ()))
    taps = [(i, j, k) for i in range(3) for j in range(3) for k in range(3)]
    for n, (i, j, k) in enumerate(taps):
        lhs = halves_in_order(flags, cs[2 - k, 2 - i : 8 - i, 3 - j : 7 - j].reshape(768, C))
        at = n * C
        rhs = jnp.concatenate([w2_own[at : at + C], w2_other[at : at + C]], axis=1)
        part = lax.dot_general(lhs, rhs, nt, preferred_element_type=F32)
        if n == 0:
            acc[...] = part
        else:
            acc[...] += part
    row = lax.broadcasted_iota(jnp.int32, (C, C), 0)
    col = lax.broadcasted_iota(jnp.int32, (C, C), 1)
    source = jnp.where(col < HALF, 2 * col, 2 * (col - HALF) + 1)
    permutation = jnp.where(row == source, 1.0, 0.0).astype(BF)
    for t in range(6):
        natural = acc[t * 128 : t * 128 + 128]
        high = natural.astype(BF)
        rest = natural - high.astype(F32)
        middle = rest.astype(BF)
        low = (rest - middle.astype(F32)).astype(BF)
        moved = [
            jnp.dot(piece, permutation, preferred_element_type=F32) for piece in (high, middle, low)
        ]
        act_grad = (moved[0] + moved[1]) + moved[2]
        here = pre[t * 128 : t * 128 + 128]
        squares = jnp.sum(here * here, axis=-1, keepdims=True)
        scale, normed, gated, sigma = normalize(here, squares, gain[...])
        norm_grad = act_grad * sigma * (1.0 + gated * (1.0 - sigma)) * gain[...]
        pre_grad = scale * (
            norm_grad - normed * jnp.mean(norm_grad * normed, axis=-1, keepdims=True)
        )
        line = lax.broadcasted_iota(jnp.int32, pre_grad.shape, 0) // W
        outside = ((line == 0) & (flags[1] == 0)) | ((line == 3) & (flags[1] == flags[4]))
        if t >= 4:
            outside = outside | (flags[0] == flags[3])
        pre_grad = jnp.where(outside, 0.0, pre_grad)
        pre_grad = halves_in_order(flags, pre_grad).astype(BF).reshape(1, 4, W, C)
        fill_shifts(ps, pre_grad, slice(t, t + 1), 0)
    for n, (i, j, k) in enumerate(taps):
        lhs = ps[2 - k, 2 - i : 6 - i, 2 - j : 4 - j].reshape(256, C)
        at = n * C
        rhs = jnp.concatenate([w1_own[at : at + C], w1_other[at : at + C]], axis=1)
        part = lax.dot_general(lhs, rhs, nt, preferred_element_type=F32)
        if n == 0:
            acc[:256] = part
        else:
            acc[:256] += part
    out[...] = acc[:256].reshape(4, 2, W, C).astype(BF)


VMEM = pl.BlockSpec(memory_space=pltpu.VMEM)
SMEM = pl.BlockSpec(memory_space=pltpu.SMEM)


def call(kernel, name, flops, out_shape, scratch, *operands):
    smem = [SMEM] if operands[0].dtype == jnp.int32 else []
    return pl.pallas_call(
        kernel,
        out_shape=out_shape,
        in_specs=smem + [VMEM] * (len(operands) - len(smem)),
        out_specs=jax.tree.map(lambda _: VMEM, out_shape),
        scratch_shapes=scratch,
        compiler_params=pltpu.CompilerParams(vmem_limit_bytes=32 * 1024 * 1024),
        cost_estimate=pl.CostEstimate(flops=flops, bytes_accessed=1 << 20, transcendentals=0),
        name=name,
    )(*operands)


def make_shifts(flags, mid, edge, other):
    shape = jax.ShapeDtypeStruct((3, 8, 8, W, C), BF)
    return call(shifts_kernel, "shifts", 1, (shape, shape), [], flags, mid, edge, other)


def forward_half(flags, xs, w1):
    shape = jax.ShapeDtypeStruct((512, HALF), F32)
    return call(half_kernel, "forward_half", 4 * 512 * ROWS * HALF, (shape, shape), [], flags, xs, w1)


def local_terms(flags, pre, own, other, gain, cs):
    shape = jax.ShapeDtypeStruct((ROWS // 2, CH), BF)
    return call(
        terms_kernel, "local_terms", 4 * 512 * ROWS * HALF, shape, [], flags, pre, own, other, gain, cs
    )


def forward_all(flags, xs, own, other):
    shape = jax.ShapeDtypeStruct((768, C), F32)
    scratch = [pltpu.VMEM((768, C), F32)]
    return call(pre_kernel, "forward_all", 2 * 768 * ROWS * C, shape, scratch, flags, xs, own, other)


def backward(flags, cs, gain, pre, w1_own, w1_other, w2_own, w2_other):
    shape = jax.ShapeDtypeStruct((4, 2, W, C), BF)
    scratch = [pltpu.VMEM((3, 6, 4, W, C), BF), pltpu.VMEM((768, C), F32)]
    return call(
        backward_kernel, "backward", 2 * 1024 * ROWS * C, shape, scratch,
        flags, cs, gain, pre, w1_own, w1_other, w2_own, w2_other,
    )


def on_device(activations, cotangent, gain, first_weight, second_weight):
    tm, rows = lax.axis_index("tm"), lax.axis_index("rows")
    core, x = rows % 2, tm // 16
    flags = jnp.stack([tm, rows, core, lax.axis_size("tm") - 1, lax.axis_size("rows") - 1])
    flags = flags.astype(jnp.int32)

    pick = lax.broadcasted_iota(jnp.int32, (C, HALF), 0) == (
        2 * lax.broadcasted_iota(jnp.int32, (C, HALF), 1) + core
    )
    half1 = jnp.dot(first_weight, pick.astype(BF), preferred_element_type=F32).astype(BF)
    half2 = lax.dynamic_slice_in_dim(second_weight, core * HALF, HALF, axis=1)
    gain_pairs = gain.reshape(HALF, 2)
    gain_half = jnp.where(core == 0, gain_pairs[:, 0], gain_pairs[:, 1]).reshape(1, HALF)
    gain_all = jnp.concatenate([gain_pairs[:, 0], gain_pairs[:, 1]]).reshape(1, C)

    w1_block = spread(half1, "tm", YZ_GROUPS).reshape(16 * 108, HALF)
    w1_blocks = [w1_block] + [from_x(w1_block, mask) for mask in (1, 2, 3)]
    w1_own = in_order(w1_blocks, x % 2 == 1, x // 2 == 1).reshape(ROWS, HALF)
    activations, cotangent, _ = lax.optimization_barrier((activations, cotangent, half1))

    nexts = shift(jnp.concatenate([activations[:2], cotangent], axis=0), "tm", -1)
    prevs = shift(activations[2:], "tm", 1)
    mid = jnp.concatenate([prevs, activations, nexts[:2], cotangent, nexts[2:]], axis=0)
    edge = beyond_chip(mid)
    next_row = jnp.where(core == 0, edge[:, 1:], edge[:, :1])
    other = swap_cores(jnp.concatenate([mid, next_row], axis=1))
    xs, cs = make_shifts(flags, mid, edge, other)

    w2_block = spread(after(half2, edge), "tm", YZ_GROUPS).reshape(16 * 108, HALF)
    xs, w2_block = lax.optimization_barrier((xs, w2_block))

    pre_half, squares = forward_half(flags, xs, w1_own)
    squares_other = swap_cores(squares)
    w2_block = after(w2_block, squares)
    w2_blocks = [w2_block] + [from_x(w2_block, mask) for mask in (1, 2, 3)]
    terms = local_terms(flags, pre_half, squares, squares_other, gain_half, cs)

    terms, w2_blocks[1] = lax.optimization_barrier((terms, w2_blocks[1]))

    total = lax.all_to_all(
        terms.reshape(4, 864, CH), "tm", 0, 0, axis_index_groups=X_GROUPS, tiled=True
    )

    w1_other = swap_cores(after(w1_own, terms))
    pre = forward_all(flags, xs, w1_own, w1_other)
    total, pre = lax.optimization_barrier((total, pre))
    w2_blocks = lax.optimization_barrier((w2_blocks, total))[0]
    w2_own = in_order(w2_blocks, x % 2 == 1, x // 2 == 1).reshape(ROWS, HALF)
    w2_other = swap_cores(w2_own)

    total = total.astype(F32).sum(0).astype(BF).reshape(16, 54, CH)
    total = lax.all_to_all(total, "tm", 0, 0, axis_index_groups=YZ_GROUPS, tiled=True)
    total = spread(total.astype(F32).sum(0), "rows", Z_GROUPS).sum(0)
    input_grad = backward(flags, cs, gain_all, pre, w1_own, w1_other, w2_own, w2_other)

    total, input_grad = lax.optimization_barrier((total, input_grad))
    other = swap_cores(total)
    even, odd = jnp.where(core == 0, total, other), jnp.where(core == 0, other, total)
    weight_grad = jnp.stack([even, odd], axis=1).reshape(108, CH)
    return (input_grad, weight_grad)


def solution(mesh):
    return jax.shard_map(
        on_device,
        mesh=mesh,
        in_specs=(
            P("tm", "rows", None, None),
            P("tm", "rows", None, None),
            P(),
            P("tm", None),
            P("tm", None),
        ),
        out_specs=(P("tm", "rows", None, None), P("tm", None)),
        check_vma=False,
    )
```

```python
import jax
import jax.numpy as jnp
from jax import lax
from jax.experimental import pallas as pl
from jax.experimental.pallas import tpu as pltpu
from jax.sharding import PartitionSpec as P

CH = 128
C = 256
W = 32
HALF = 128
ROWS = 6912
EPS = 1e-06
BF = jnp.bfloat16
F32 = jnp.float32

YZ_GROUPS = [[x * 16 + k for k in range(16)] for x in range(4)]
X_GROUPS = [[k, k + 16, k + 32, k + 48] for k in range(16)]
Y_GROUPS = [[b * 8 + k for k in range(8)] for b in range(8)]
ROW_GROUPS = [list(range(8))]


def spread(block, axis, groups):
    count = len(groups[0])
    operand = jnp.broadcast_to(block[None], (count,) + block.shape)
    return lax.all_to_all(operand, axis, 0, 0, axis_index_groups=groups, tiled=True)


def swap_cores(block):
    return lax.ppermute(block, "rows", [(i, i ^ 1) for i in range(lax.axis_size("rows"))])


def shift(block, axis, distance):
    count = lax.axis_size(axis)
    route = [(i, i + distance) for i in range(count) if 0 <= i + distance < count]
    return lax.ppermute(block, axis, route)


def from_z(block, distance):
    def device(x, y, z, c):
        return (x * 16 + (z % 2) * 8 + y) * 8 + (z // 2) * 2 + c

    route = [
        (device(x, y, (z + distance) % 8, c), device(x, y, z, c))
        for x in range(4)
        for y in range(8)
        for z in range(8)
        for c in range(2)
    ]
    return lax.ppermute(block, ("tm", "rows"), route)


def beyond_chip(block):
    count = lax.axis_size("rows")
    route = [(i - 1, i) for i in range(2, count, 2)] + [(i + 1, i) for i in range(1, count - 1, 2)]
    return lax.ppermute(block, "rows", route)


def after(value, *others):
    return lax.optimization_barrier((value,) + others)[0]


def fill_shifts(out, piece, frames, at):
    count, rows = piece.shape[:2]
    flat = piece.reshape(count * rows * W, piece.shape[3]).astype(F32)
    column = lax.broadcasted_iota(jnp.int32, flat.shape, 0) % W
    before = jnp.where(column == 0, 0.0, pltpu.roll(flat, 1, 0))
    behind = jnp.where(column == W - 1, 0.0, pltpu.roll(flat, flat.shape[0] - 1, 0))
    out[1, frames, pl.ds(at, rows)] = piece
    out[0, frames, pl.ds(at, rows)] = before.astype(BF).reshape(piece.shape)
    out[2, frames, pl.ds(at, rows)] = behind.astype(BF).reshape(piece.shape)


def normalize(pre, squares, gain):
    scale = lax.rsqrt(squares * (1.0 / C) + EPS)
    normed = pre * scale
    gated = normed * gain
    sigma = 1.0 / (1.0 + jnp.exp(-gated))
    return scale, normed, gated, sigma


def fill_all(out, flags, field, base, count, far, channels=C):
    mid, edge, other = field
    core = flags[2]
    for f in range(0, count, 2):
        frames = slice(f, f + 2)
        source = slice(base + f, base + f + 2)
        fill_shifts(out, mid[source, :, :, :channels], frames, 3)
        fill_shifts(out, edge[source, :, :, :channels], frames, 1 + 4 * core)
        fill_shifts(out, other[source, :2, :, :channels], frames, 5 - 4 * core)
        if far:
            fill_shifts(out, other[source, 2:, :, :channels], frames, 0)
            for k in range(3):
                out[k, frames, 7:8] = out[k, frames, 0:1]


def arrange(out, flags, part, more_a, more_b):
    here, there = flags[5] * 864, 864 - flags[5] * 864
    for n in range(4):
        out[pl.ds(pl.multiple_of(n * 1728 + here, 32), 864)] = part[n]
        more = more_a[n] if n < 2 else more_b[n - 2]
        out[pl.ds(pl.multiple_of(n * 1728 + there, 32), 864)] = more


def half_kernel(flags, mid, edge, other, part, more_a, more_b, pre, squares, w1, xs):
    base = 2 - 2 * flags[2]
    fill_all(xs, flags, (mid, edge, other), 0, 6, True)
    arrange(w1, flags, part, more_a, more_b)
    for i in range(3):
        for j in range(3):
            lhs = jnp.concatenate(
                [xs[k, i : i + 4, pl.ds(base + j, 4)].reshape(512, C) for k in range(3)], axis=1
            )
            at = (i * 3 + j) * 3 * C
            part = jnp.dot(lhs, w1[at : at + 3 * C], preferred_element_type=F32)
            if i == 0 and j == 0:
                pre[...] = part
            else:
                pre[...] += part
    total = jnp.sum(pre[...] * pre[...], axis=1, keepdims=True)
    squares[...] = jnp.broadcast_to(total, (512, HALF))


def terms_kernel(flags, pre, own, others, gain, mid, edge, other, out, cs):
    base = 2 - 2 * flags[2]
    fill_all(cs, flags, (mid, edge, other), 8, 6, True, CH)
    _, _, gated, sigma = normalize(pre[...], own[...] + others[...], gain[...])
    act = (gated * sigma).T.astype(BF)
    taps = [(i, j, k) for i in range(3) for j in range(3) for k in range(3)]

    def operand(i, j, k):
        return cs[2 - k, 2 - i : 6 - i, pl.ds(base + 2 - j, 4)].reshape(512, CH)

    for n in range(0, 27, 2):
        pair = taps[n : n + 2]
        rhs = jnp.concatenate([operand(*tap) for tap in pair], axis=1)
        term = jnp.dot(act, rhs, preferred_element_type=F32).astype(BF)
        for m in range(len(pair)):
            out[(n + m) * HALF : (n + m + 1) * HALF] = term[:, m * CH : (m + 1) * CH]


def halves_in_order(flags, value):
    turned = jnp.concatenate([value[..., HALF:], value[..., :HALF]], axis=-1)
    return jnp.where(flags[2] == 1, turned, value)


def pre_kernel(flags, mid, edge, others, own, other, pre, acc, xs):
    fill_all(xs, flags, (mid, edge, others), 0, 8, False)
    for i in range(3):
        for j in range(3):
            lhs = jnp.concatenate(
                [xs[k, i : i + 6, j + 1 : j + 5].reshape(768, C) for k in range(3)], axis=1
            )
            at = (i * 3 + j) * 3 * C
            rhs = jnp.concatenate([own[at : at + 3 * C], other[at : at + 3 * C]], axis=1)
            part = jnp.dot(lhs, rhs, preferred_element_type=F32)
            if i == 0 and j == 0:
                acc[...] = part
            else:
                acc[...] += part
    pre[...] = halves_in_order(flags, acc[...])


def backward_kernel(
    flags, mid, edge, other, gain, pre, w1_own, w1_other, part, more_a, more_b,
    far_part, far_more_a, far_more_b, out, ps, acc, cs, w2_own, w2_other,
):
    fill_all(cs, flags, (mid, edge, other), 8, 8, False)
    arrange(w2_own, flags, part, more_a, more_b)
    arrange(w2_other, flags, far_part, far_more_a, far_more_b)
    nt = (((1,), (1,)), ((), ()))
    taps = [(i, j, k) for i in range(3) for j in range(3) for k in range(3)]
    for n, (i, j, k) in enumerate(taps):
        lhs = halves_in_order(flags, cs[2 - k, 2 - i : 8 - i, 3 - j : 7 - j].reshape(768, C))
        at = n * C
        rhs = jnp.concatenate([w2_own[at : at + C], w2_other[at : at + C]], axis=1)
        part = lax.dot_general(lhs, rhs, nt, preferred_element_type=F32)
        if n == 0:
            acc[...] = part
        else:
            acc[...] += part
    row = lax.broadcasted_iota(jnp.int32, (C, C), 0)
    col = lax.broadcasted_iota(jnp.int32, (C, C), 1)
    source = jnp.where(col < HALF, 2 * col, 2 * (col - HALF) + 1)
    permutation = jnp.where(row == source, 1.0, 0.0).astype(BF)
    for t in range(6):
        natural = acc[t * 128 : t * 128 + 128]
        high = natural.astype(BF)
        rest = natural - high.astype(F32)
        middle = rest.astype(BF)
        low = (rest - middle.astype(F32)).astype(BF)
        moved = [
            jnp.dot(piece, permutation, preferred_element_type=F32) for piece in (high, middle, low)
        ]
        act_grad = (moved[0] + moved[1]) + moved[2]
        here = pre[t * 128 : t * 128 + 128]
        squares = jnp.sum(here * here, axis=-1, keepdims=True)
        scale, normed, gated, sigma = normalize(here, squares, gain[...])
        norm_grad = act_grad * sigma * (1.0 + gated * (1.0 - sigma)) * gain[...]
        pre_grad = scale * (
            norm_grad - normed * jnp.mean(norm_grad * normed, axis=-1, keepdims=True)
        )
        line = lax.broadcasted_iota(jnp.int32, pre_grad.shape, 0) // W
        outside = ((line == 0) & (flags[1] == 0)) | ((line == 3) & (flags[1] == flags[4]))
        if t >= 4:
            outside = outside | (flags[0] == flags[3])
        pre_grad = jnp.where(outside, 0.0, pre_grad)
        pre_grad = halves_in_order(flags, pre_grad).astype(BF).reshape(1, 4, W, C)
        fill_shifts(ps, pre_grad, slice(t, t + 1), 0)
    for n, (i, j, k) in enumerate(taps):
        lhs = ps[2 - k, 2 - i : 6 - i, 2 - j : 4 - j].reshape(256, C)
        at = n * C
        rhs = jnp.concatenate([w1_own[at : at + C], w1_other[at : at + C]], axis=1)
        part = lax.dot_general(lhs, rhs, nt, preferred_element_type=F32)
        if n == 0:
            acc[:256] = part
        else:
            acc[:256] += part
    out[...] = acc[:256].reshape(4, 2, W, C).astype(BF)


VMEM = pl.BlockSpec(memory_space=pltpu.VMEM)
SMEM = pl.BlockSpec(memory_space=pltpu.SMEM)


def call(kernel, name, flops, out_shape, scratch, *operands):
    smem = [SMEM] if operands[0].dtype == jnp.int32 else []
    return pl.pallas_call(
        kernel,
        out_shape=out_shape,
        in_specs=smem + [VMEM] * (len(operands) - len(smem)),
        out_specs=jax.tree.map(lambda _: VMEM, out_shape),
        scratch_shapes=scratch,
        compiler_params=pltpu.CompilerParams(vmem_limit_bytes=32 * 1024 * 1024),
        cost_estimate=pl.CostEstimate(flops=flops, bytes_accessed=1 << 20, transcendentals=0),
        name=name,
    )(*operands)


def forward_half(flags, field, part, more_a, more_b):
    shape = jax.ShapeDtypeStruct((512, HALF), F32)
    weight = jax.ShapeDtypeStruct((ROWS, HALF), BF)
    scratch = [pltpu.VMEM((3, 6, 8, W, C), BF)]
    return call(
        half_kernel, "forward_half", 4 * 512 * ROWS * HALF, (shape, shape, weight), scratch,
        flags, *field, part, more_a, more_b,
    )


def local_terms(flags, pre, own, others, gain, field):
    shape = jax.ShapeDtypeStruct((ROWS // 2, CH), BF)
    scratch = [pltpu.VMEM((3, 6, 8, W, CH), BF)]
    return call(
        terms_kernel, "local_terms", 4 * 512 * ROWS * HALF, shape, scratch,
        flags, pre, own, others, gain, *field,
    )


def forward_all(flags, field, own, other):
    shape = jax.ShapeDtypeStruct((768, C), F32)
    scratch = [pltpu.VMEM((768, C), F32), pltpu.VMEM((3, 8, 8, W, C), BF)]
    return call(
        pre_kernel, "forward_all", 2 * 768 * ROWS * C, shape, scratch, flags, *field, own, other
    )


def backward(flags, field, gain, pre, w1_own, w1_other, w2_own, w2_other):
    shape = jax.ShapeDtypeStruct((4, 2, W, C), BF)
    scratch = [
        pltpu.VMEM((3, 6, 4, W, C), BF),
        pltpu.VMEM((768, C), F32),
        pltpu.VMEM((3, 8, 8, W, C), BF),
        pltpu.VMEM((ROWS, HALF), BF),
        pltpu.VMEM((ROWS, HALF), BF),
    ]
    return call(
        backward_kernel, "backward", 2 * 1024 * ROWS * C, shape, scratch,
        flags, *field, gain, pre, w1_own, w1_other, *w2_own, *w2_other,
    )


def on_device(activations, cotangent, gain, first_weight, second_weight):
    tm, rows = lax.axis_index("tm"), lax.axis_index("rows")
    core, z_lo = rows % 2, (tm // 8) % 2
    flags = jnp.stack([tm, rows, core, lax.axis_size("tm") - 1, lax.axis_size("rows") - 1, z_lo])
    flags = flags.astype(jnp.int32)

    pick = lax.broadcasted_iota(jnp.int32, (C, HALF), 0) == (
        2 * lax.broadcasted_iota(jnp.int32, (C, HALF), 1) + core
    )
    half1 = jnp.dot(first_weight, pick.astype(BF), preferred_element_type=F32).astype(BF)
    half2 = lax.dynamic_slice_in_dim(second_weight, core * HALF, HALF, axis=1)
    gain_pairs = gain.reshape(HALF, 2)
    gain_half = jnp.where(core == 0, gain_pairs[:, 0], gain_pairs[:, 1]).reshape(1, HALF)
    gain_all = jnp.concatenate([gain_pairs[:, 0], gain_pairs[:, 1]]).reshape(1, C)

    block = spread(jnp.concatenate([half1, half2]), "tm", Y_GROUPS)
    w1_part = spread(block[:, :108].reshape(864, HALF), "tm", X_GROUPS)
    activations, cotangent, _ = lax.optimization_barrier((activations, cotangent, half1))

    nexts = shift(jnp.concatenate([activations[:2], cotangent], axis=0), "tm", -1)
    prevs = shift(activations[2:], "tm", 1)
    mid = jnp.concatenate([prevs, activations, nexts[:2], cotangent, nexts[2:]], axis=0)
    edge = beyond_chip(mid)
    next_row = jnp.where(core == 0, edge[:, 1:], edge[:, :1])
    field = (mid, edge, swap_cores(jnp.concatenate([mid, next_row], axis=1)))

    w1_more = from_z(w1_part[:2], 1), from_z(w1_part[2:], -1)
    w2_part = spread(after(block[:, 108:].reshape(864, HALF), w1_part), "tm", X_GROUPS)
    w1_more, w2_part = lax.optimization_barrier((w1_more, w2_part))

    pre_half, squares, w1_own = forward_half(flags, field, w1_part, *w1_more)
    squares_other = swap_cores(squares)
    terms = local_terms(flags, pre_half, squares, squares_other, gain_half, field)

    total = lax.all_to_all(
        terms.reshape(4, 864, CH), "tm", 0, 0, axis_index_groups=X_GROUPS, tiled=True
    )
    w2_part = after(w2_part, terms)
    w2_own = [w2_part, from_z(w2_part[:2], 1), from_z(w2_part[2:], -1)]
    w1_other = swap_cores(after(w1_own, terms))
    pre = forward_all(flags, field, w1_own, w1_other)
    total, pre = lax.optimization_barrier((total, pre))
    w2_other = [swap_cores(part) for part in w2_own]
    input_grad = backward(flags, field, gain_all, pre, w1_own, w1_other, w2_own, w2_other)

    total = total.astype(F32).sum(0).astype(BF).reshape(16, 54, CH)
    total = lax.all_to_all(total, "tm", 0, 0, axis_index_groups=YZ_GROUPS, tiled=True)
    total = spread(total.astype(F32).sum(0), "rows", ROW_GROUPS)
    total, input_grad = lax.optimization_barrier((total, input_grad))
    weight_grad = total.reshape(4, 2, 54, CH).sum(0).transpose(1, 0, 2).reshape(108, CH)
    return (input_grad, weight_grad)


def solution(mesh):
    return jax.shard_map(
        on_device,
        mesh=mesh,
        in_specs=(
            P("tm", "rows", None, None),
            P("tm", "rows", None, None),
            P(),
            P("tm", None),
            P("tm", None),
        ),
        out_specs=(P("tm", "rows", None, None), P("tm", None)),
        check_vma=False,
    )
```

```python
import jax
import jax.numpy as jnp
from jax import lax
from jax.experimental import pallas as pl
from jax.experimental.pallas import tpu as pltpu
from jax.sharding import PartitionSpec as P

CH = 128
C = 256
W = 32
HALF = 128
ROWS = 6912
EPS = 1e-06
BF = jnp.bfloat16
F32 = jnp.float32

YZ_GROUPS = [[x * 16 + k for k in range(16)] for x in range(4)]
X_GROUPS = [[k, k + 16, k + 32, k + 48] for k in range(16)]
Y_GROUPS = [[b * 8 + k for k in range(8)] for b in range(8)]
ROW_GROUPS = [list(range(8))]
UNPACK_COST = 1 << 36
SUM_COST = 1 << 20
SPLIT_COST = 1 << 36
GAINS_COST = 1 << 36


def spread(block, axis, groups):
    count = len(groups[0])
    operand = jnp.broadcast_to(block[None], (count,) + block.shape)
    return lax.all_to_all(operand, axis, 0, 0, axis_index_groups=groups, tiled=True)


def swap_cores(block):
    return lax.ppermute(block, "rows", [(i, i ^ 1) for i in range(lax.axis_size("rows"))])


def shift(block, axis, distance):
    count = lax.axis_size(axis)
    route = [(i, i + distance) for i in range(count) if 0 <= i + distance < count]
    return lax.ppermute(block, axis, route)


def from_z(block, distance):
    def device(x, y, z, c):
        return (x * 16 + (z % 2) * 8 + y) * 8 + (z // 2) * 2 + c

    route = [
        (device(x, y, (z + distance) % 8, c), device(x, y, z, c))
        for x in range(4)
        for y in range(8)
        for z in range(8)
        for c in range(2)
    ]
    return lax.ppermute(block, ("tm", "rows"), route)


def beyond_chip(block):
    count = lax.axis_size("rows")
    route = [(i - 1, i) for i in range(2, count, 2)] + [(i + 1, i) for i in range(1, count - 1, 2)]
    return lax.ppermute(block, "rows", route)


def after(value, *others):
    return lax.optimization_barrier((value,) + others)[0]


def fill_shifts(out, piece, frames, at):
    count, rows = piece.shape[:2]
    flat = piece.reshape(count * rows * W, piece.shape[3]).astype(F32)
    column = lax.broadcasted_iota(jnp.int32, flat.shape, 0) % W
    before = jnp.where(column == 0, 0.0, pltpu.roll(flat, 1, 0))
    behind = jnp.where(column == W - 1, 0.0, pltpu.roll(flat, flat.shape[0] - 1, 0))
    out[1, frames, pl.ds(at, rows)] = piece
    out[0, frames, pl.ds(at, rows)] = before.astype(BF).reshape(piece.shape)
    out[2, frames, pl.ds(at, rows)] = behind.astype(BF).reshape(piece.shape)


def normalize(pre, squares, gain):
    scale = lax.rsqrt(squares * (1.0 / C) + EPS)
    normed = pre * scale
    gated = normed * gain
    sigma = 1.0 / (1.0 + jnp.exp(-gated))
    return scale, normed, gated, sigma


def fill_all(out, flags, field, base, count, far, channels=C):
    mid, edge, other = field
    core = flags[2]
    for f in range(0, count, 2):
        frames = slice(f, f + 2)
        source = slice(base + f, base + f + 2)
        fill_shifts(out, mid[source, :, :, :channels], frames, 3)
        fill_shifts(out, edge[source, :, :, :channels], frames, 1 + 4 * core)
        fill_shifts(out, other[source, :2, :, :channels], frames, 5 - 4 * core)
        if far:
            fill_shifts(out, other[source, 2:, :, :channels], frames, 0)
            for k in range(3):
                out[k, frames, 7:8] = out[k, frames, 0:1]


def start_all(sems, pairs):
    copies = [pltpu.make_async_copy(source, to, sems.at[n]) for n, (source, to) in enumerate(pairs)]
    for copy in copies:
        copy.start()
    return copies


def wait_all(copies):
    for copy in copies:
        copy.wait()


def fetch(out, flags, weight, sems):
    here, there = flags[5] * 864, 864 - flags[5] * 864
    pairs = []
    for n in range(4):
        more = weight[1].at[n] if len(weight) == 2 else weight[1 + n // 2].at[n % 2]
        pairs.append((weight[0].at[n], out.at[pl.ds(pl.multiple_of(n * 1728 + here, 32), 864)]))
        pairs.append((more, out.at[pl.ds(pl.multiple_of(n * 1728 + there, 32), 864)]))
    return start_all(sems, pairs)


def gains_kernel(flags, gain, half, both):
    row = lax.broadcasted_iota(jnp.int32, (C, HALF), 0)
    col = lax.broadcasted_iota(jnp.int32, (C, HALF), 1)
    wide = jnp.broadcast_to(gain[...], (HALF, C)).T
    even = jnp.sum(jnp.where(row == 2 * col, wide, 0.0), axis=0, keepdims=True)
    odd = jnp.sum(jnp.where(row == 2 * col + 1, wide, 0.0), axis=0, keepdims=True)
    half[...] = jnp.where(flags[2] == 0, even, odd)
    both[...] = jnp.concatenate([even, odd], axis=1)


def unpack_kernel(block_in, first, second, block, sems):
    wait_all(start_all(sems, ((block_in, block),)))
    for out, at in ((first, 0), (second, 108)):
        rows = [block[n, at : at + 108].astype(F32) for n in range(8)]
        rows = jnp.concatenate(rows, axis=0).astype(BF)
        for n in range(4):
            out[n] = rows


def split_kernel(part, first, second, sems):
    wait_all(start_all(sems, ((part.at[:2], first), (part.at[2:], second))))


def sum_kernel(terms_in, out, terms, sems):
    wait_all(start_all(sems, ((terms_in, terms),)))
    total = terms[0].astype(F32) + terms[1].astype(F32)
    total = (total + terms[2].astype(F32)) + terms[3].astype(F32)
    for n in range(16):
        out[n] = total[n * 54 : n * 54 + 54].astype(BF)


def half_kernel(flags, mid, edge, other, part, more_a, more_b, pre, squares, w1, xs, sems):
    base = 2 - 2 * flags[2]
    copies = fetch(w1, flags, (part, more_a, more_b), sems)
    fill_all(xs, flags, (mid, edge, other), 0, 6, True)
    wait_all(copies)
    for i in range(3):
        for j in range(3):
            lhs = jnp.concatenate(
                [xs[k, i : i + 4, pl.ds(base + j, 4)].reshape(512, C) for k in range(3)], axis=1
            )
            at = (i * 3 + j) * 3 * C
            part = jnp.dot(lhs, w1[at : at + 3 * C], preferred_element_type=F32)
            if i == 0 and j == 0:
                pre[...] = part
            else:
                pre[...] += part
    total = jnp.sum(pre[...] * pre[...], axis=1, keepdims=True)
    squares[...] = jnp.broadcast_to(total, (512, HALF))


def terms_kernel(
    flags, pre_in, own_in, others_in, gain, mid, edge, other, out, cs, pre, own, others, sems
):
    base = 2 - 2 * flags[2]
    copies = start_all(sems, ((pre_in, pre), (own_in, own), (others_in, others)))
    fill_all(cs, flags, (mid, edge, other), 8, 6, True, CH)
    wait_all(copies)
    _, _, gated, sigma = normalize(pre[...], own[...] + others[...], gain[...])
    act = (gated * sigma).T.astype(BF)
    taps = [(i, j, k) for i in range(3) for j in range(3) for k in range(3)]

    def operand(i, j, k):
        return cs[2 - k, 2 - i : 6 - i, pl.ds(base + 2 - j, 4)].reshape(512, CH)

    for n in range(0, 27, 2):
        pair = taps[n : n + 2]
        rhs = jnp.concatenate([operand(*tap) for tap in pair], axis=1)
        term = jnp.dot(act, rhs, preferred_element_type=F32).astype(BF)
        for m in range(len(pair)):
            out[(n + m) * HALF : (n + m + 1) * HALF] = term[:, m * CH : (m + 1) * CH]


def halves_in_order(flags, value):
    turned = jnp.concatenate([value[..., HALF:], value[..., :HALF]], axis=-1)
    return jnp.where(flags[2] == 1, turned, value)


def pre_kernel(
    flags, mid, edge, others, part, more_a, more_b, far_part, far_more, pre, acc, xs, own, other, sems
):
    copies = fetch(own, flags, (part, more_a, more_b), sems.at[0])
    copies += fetch(other, flags, (far_part, far_more), sems.at[1])
    fill_all(xs, flags, (mid, edge, others), 0, 8, False)
    wait_all(copies)
    for i in range(3):
        for j in range(3):
            lhs = jnp.concatenate(
                [xs[k, i : i + 6, j + 1 : j + 5].reshape(768, C) for k in range(3)], axis=1
            )
            at = (i * 3 + j) * 3 * C
            rhs = jnp.concatenate([own[at : at + 3 * C], other[at : at + 3 * C]], axis=1)
            part = jnp.dot(lhs, rhs, preferred_element_type=F32)
            if i == 0 and j == 0:
                acc[...] = part
            else:
                acc[...] += part
    pre[...] = halves_in_order(flags, acc[...])


def middle_kernel(
    flags, mid, edge, other, gain, pre_in, part, more_a, more_b, far_part, far_more_a, far_more_b,
    out, pre, acc, cs, w2_own, w2_other, sems, pre_sem,
):
    copies = fetch(w2_own, flags, (part, more_a, more_b), sems.at[0])
    copies += fetch(w2_other, flags, (far_part, far_more_a, far_more_b), sems.at[1])
    copies += start_all(pre_sem, ((pre_in, pre),))
    fill_all(cs, flags, (mid, edge, other), 8, 8, False)
    wait_all(copies)
    nt = (((1,), (1,)), ((), ()))
    taps = [(i, j, k) for i in range(3) for j in range(3) for k in range(3)]
    for n, (i, j, k) in enumerate(taps):
        lhs = halves_in_order(flags, cs[2 - k, 2 - i : 8 - i, 3 - j : 7 - j].reshape(768, C))
        at = n * C
        rhs = jnp.concatenate([w2_own[at : at + C], w2_other[at : at + C]], axis=1)
        part = lax.dot_general(lhs, rhs, nt, preferred_element_type=F32)
        if n == 0:
            acc[...] = part
        else:
            acc[...] += part
    row = lax.broadcasted_iota(jnp.int32, (C, C), 0)
    col = lax.broadcasted_iota(jnp.int32, (C, C), 1)
    source = jnp.where(col < HALF, 2 * col, 2 * (col - HALF) + 1)
    permutation = jnp.where(row == source, 1.0, 0.0).astype(BF)
    for t in range(6):
        natural = acc[t * 128 : t * 128 + 128]
        high = natural.astype(BF)
        rest = natural - high.astype(F32)
        middle = rest.astype(BF)
        low = (rest - middle.astype(F32)).astype(BF)
        moved = [
            jnp.dot(piece, permutation, preferred_element_type=F32) for piece in (high, middle, low)
        ]
        act_grad = (moved[0] + moved[1]) + moved[2]
        here = pre[t * 128 : t * 128 + 128]
        squares = jnp.sum(here * here, axis=-1, keepdims=True)
        scale, normed, gated, sigma = normalize(here, squares, gain[...])
        norm_grad = act_grad * sigma * (1.0 + gated * (1.0 - sigma)) * gain[...]
        pre_grad = scale * (
            norm_grad - normed * jnp.mean(norm_grad * normed, axis=-1, keepdims=True)
        )
        line = lax.broadcasted_iota(jnp.int32, pre_grad.shape, 0) // W
        outside = ((line == 0) & (flags[1] == 0)) | ((line == 3) & (flags[1] == flags[4]))
        if t >= 4:
            outside = outside | (flags[0] == flags[3])
        pre_grad = jnp.where(outside, 0.0, pre_grad)
        out[t] = halves_in_order(flags, pre_grad).astype(BF).reshape(4, W, C)


def last_kernel(
    flags, grad, part, more_a, more_b, far_part, far_more, out, ps, acc, w1_own, w1_other, sems
):
    copies = fetch(w1_own, flags, (part, more_a, more_b), sems.at[0])
    copies += fetch(w1_other, flags, (far_part, far_more), sems.at[1])
    for t in range(0, 6, 2):
        fill_shifts(ps, grad[t : t + 2], slice(t, t + 2), 0)
    wait_all(copies)
    nt = (((1,), (1,)), ((), ()))
    taps = [(i, j, k) for i in range(3) for j in range(3) for k in range(3)]
    for n, (i, j, k) in enumerate(taps):
        lhs = ps[2 - k, 2 - i : 6 - i, 2 - j : 4 - j].reshape(256, C)
        at = n * C
        rhs = jnp.concatenate([w1_own[at : at + C], w1_other[at : at + C]], axis=1)
        part = lax.dot_general(lhs, rhs, nt, preferred_element_type=F32)
        if n == 0:
            acc[:256] = part
        else:
            acc[:256] += part
    out[...] = acc[:256].reshape(4, 2, W, C).astype(BF)


VMEM = pl.BlockSpec(memory_space=pltpu.VMEM)
SMEM = pl.BlockSpec(memory_space=pltpu.SMEM)
ANY = pl.BlockSpec(memory_space=pl.ANY)
WEIGHT = pltpu.VMEM((ROWS, HALF), BF)
SEMS = pltpu.SemaphoreType.DMA


def call(kernel, name, flops, out_shape, scratch, specs, *operands):
    return pl.pallas_call(
        kernel,
        out_shape=out_shape,
        in_specs=specs,
        out_specs=jax.tree.map(lambda _: VMEM, out_shape),
        scratch_shapes=scratch,
        compiler_params=pltpu.CompilerParams(vmem_limit_bytes=32 * 1024 * 1024),
        cost_estimate=pl.CostEstimate(flops=flops, bytes_accessed=1 << 20, transcendentals=0),
        name=name,
    )(*operands)


def order_gains(flags, gain):
    half = jax.ShapeDtypeStruct((1, HALF), F32)
    both = jax.ShapeDtypeStruct((1, C), F32)
    specs = [SMEM, VMEM]
    return call(gains_kernel, "gains", GAINS_COST, (half, both), [], specs, flags, gain.reshape(1, C))


def unpack(block):
    shape = jax.ShapeDtypeStruct((4, 864, HALF), BF)
    scratch = [pltpu.VMEM((8, 216, HALF), BF), SEMS((1,))]
    return call(unpack_kernel, "unpack", UNPACK_COST, (shape, shape), scratch, [ANY], block)


def split(part):
    shape = jax.ShapeDtypeStruct((2, 864, HALF), BF)
    return call(split_kernel, "split", SPLIT_COST, (shape, shape), [SEMS((2,))], [ANY], part)


def sum_terms(terms):
    shape = jax.ShapeDtypeStruct((16, 54, CH), BF)
    scratch = [pltpu.VMEM((4, 864, CH), BF), SEMS((1,))]
    return call(sum_kernel, "sum_terms", SUM_COST, shape, scratch, [ANY], terms)


def forward_half(flags, field, weight):
    shape = jax.ShapeDtypeStruct((512, HALF), F32)
    scratch = [WEIGHT, pltpu.VMEM((3, 6, 8, W, C), BF), SEMS((8,))]
    return call(
        half_kernel, "forward_half", 4 * 512 * ROWS * HALF, (shape, shape), scratch,
        [SMEM] + [VMEM] * 3 + [ANY] * 3, flags, *field, *weight,
    )


def local_terms(flags, pre, own, others, gain, field):
    shape = jax.ShapeDtypeStruct((ROWS // 2, CH), BF)
    scratch = [pltpu.VMEM((3, 6, 8, W, CH), BF)] + [pltpu.VMEM((512, HALF), F32)] * 3 + [SEMS((3,))]
    return call(
        terms_kernel, "local_terms", 4 * 512 * ROWS * HALF, shape, scratch,
        [SMEM] + [ANY] * 3 + [VMEM] * 4, flags, pre, own, others, gain, *field,
    )


def forward_all(flags, field, own, other):
    shape = jax.ShapeDtypeStruct((768, C), F32)
    scratch = [
        pltpu.VMEM((768, C), F32), pltpu.VMEM((3, 8, 8, W, C), BF), WEIGHT, WEIGHT, SEMS((2, 8))
    ]
    return call(
        pre_kernel, "forward_all", 2 * 768 * ROWS * C, shape, scratch,
        [SMEM] + [VMEM] * 3 + [ANY] * 5, flags, *field, *own, *other,
    )


def middle(flags, field, gain, pre, own, other):
    shape = jax.ShapeDtypeStruct((6, 4, W, C), BF)
    scratch = [
        pltpu.VMEM((768, C), F32), pltpu.VMEM((768, C), F32), pltpu.VMEM((3, 8, 8, W, C), BF),
        WEIGHT, WEIGHT, SEMS((2, 8)), SEMS((1,)),
    ]
    return call(
        middle_kernel, "middle", 2 * 768 * ROWS * C, shape, scratch,
        [SMEM] + [VMEM] * 4 + [ANY] * 7, flags, *field, gain, pre, *own, *other,
    )


def last(flags, grad, own, other):
    shape = jax.ShapeDtypeStruct((4, 2, W, C), BF)
    scratch = [
        pltpu.VMEM((3, 6, 4, W, C), BF), pltpu.VMEM((256, C), F32), WEIGHT, WEIGHT, SEMS((2, 8))
    ]
    return call(
        last_kernel, "last", 2 * 256 * ROWS * C, shape, scratch,
        [SMEM, VMEM] + [ANY] * 5, flags, grad, *own, *other,
    )


def on_device(activations, cotangent, gain, first_weight, second_weight):
    tm, rows = lax.axis_index("tm"), lax.axis_index("rows")
    core, z_lo = rows % 2, (tm // 8) % 2
    flags = jnp.stack([tm, rows, core, lax.axis_size("tm") - 1, lax.axis_size("rows") - 1, z_lo])
    flags = flags.astype(jnp.int32)

    pick = lax.broadcasted_iota(jnp.int32, (C, HALF), 0) == (
        2 * lax.broadcasted_iota(jnp.int32, (C, HALF), 1) + core
    )
    half1 = jnp.dot(first_weight, pick.astype(BF), preferred_element_type=F32).astype(BF)
    half2 = lax.dynamic_slice_in_dim(second_weight, core * HALF, HALF, axis=1)

    halves = jnp.concatenate([half1, half2])
    halves = jnp.broadcast_to(halves[None], (8,) + halves.shape)
    block = lax.all_to_all(halves, "tm", 0, 0, axis_index_groups=Y_GROUPS, tiled=True)
    w1_block, w2_block = unpack(block)
    w1_part = lax.all_to_all(w1_block, "tm", 0, 0, axis_index_groups=X_GROUPS, tiled=True)
    activations, cotangent, _ = lax.optimization_barrier((activations, cotangent, halves))

    nexts = shift(jnp.concatenate([activations[:2], cotangent], axis=0), "tm", -1)
    prevs = shift(activations[2:], "tm", 1)
    gains = order_gains(flags, gain)
    nexts, prevs, gains = lax.optimization_barrier((nexts, prevs, gains))
    gain_half, gain_all = gains
    mid = jnp.concatenate([prevs, activations, nexts[:2], cotangent, nexts[2:]], axis=0)
    edge = beyond_chip(mid)
    next_row = jnp.where(core == 0, edge[:, 1:], edge[:, :1])
    other = swap_cores(jnp.concatenate([mid, next_row], axis=1))
    field = (mid, edge, other)

    first, second = split(w1_part)
    w1_more = [from_z(first, 1), from_z(second, -1)]
    w1_far = [swap_cores(w1_part)]
    w2_part = lax.all_to_all(
        after(w2_block, w1_more[0]), "tm", 0, 0, axis_index_groups=X_GROUPS, tiled=True
    )

    w1_own = [w1_part] + w1_more
    pre_half, squares = forward_half(flags, field, w1_own)
    squares_other = swap_cores(squares)
    squares_other, w2_part = lax.optimization_barrier((squares_other, w2_part))
    terms = local_terms(flags, pre_half, squares, squares_other, gain_half, field)

    total = lax.all_to_all(
        terms.reshape(4, 864, CH), "tm", 0, 0, axis_index_groups=X_GROUPS, tiled=True
    )
    w1_far.append(swap_cores(after(jnp.concatenate(w1_more), terms)))
    w2_part = after(w2_part, terms)
    w2_own = [w2_part, from_z(w2_part[:2], 1), from_z(w2_part[2:], -1)]
    pre = forward_all(flags, field, w1_own, w1_far)
    total, pre = lax.optimization_barrier((total, pre))
    w2_far = [swap_cores(part) for part in w2_own]
    pre_grad = middle(flags, field, gain_all, pre, w2_own, w2_far)

    total = lax.all_to_all(sum_terms(total), "tm", 0, 0, axis_index_groups=YZ_GROUPS, tiled=True)
    total = spread(total.astype(F32).sum(0), "rows", ROW_GROUPS)
    input_grad = last(flags, pre_grad, w1_own, w1_far)
    total, input_grad = lax.optimization_barrier((total, input_grad))
    weight_grad = total.reshape(4, 2, 54, CH).sum(0).transpose(1, 0, 2).reshape(108, CH)
    return (input_grad, weight_grad)


def solution(mesh):
    return jax.shard_map(
        on_device,
        mesh=mesh,
        in_specs=(
            P("tm", "rows", None, None),
            P("tm", "rows", None, None),
            P(),
            P("tm", None),
            P("tm", None),
        ),
        out_specs=(P("tm", "rows", None, None), P("tm", None)),
        check_vma=False,
    )
```

```python
import jax
import jax.numpy as jnp
from jax import lax
from jax.experimental import pallas as pl
from jax.experimental.pallas import tpu as pltpu
from jax.sharding import PartitionSpec as P

CH = 128
C = 256
W = 32
HALF = 128
ROWS = 6912
EPS = 1e-06
BF = jnp.bfloat16
F32 = jnp.float32

YZ_GROUPS = [[x * 16 + k for k in range(16)] for x in range(4)]
X_GROUPS = [[k, k + 16, k + 32, k + 48] for k in range(16)]
ROW_GROUPS = [list(range(8))]
GAINS_COST = 1 << 36
UNPACK_COST = 1 << 36
ASSEMBLE_COST = 1 << 36


def spread(block, axis, groups):
    count = len(groups[0])
    operand = jnp.broadcast_to(block[None], (count,) + block.shape)
    return lax.all_to_all(operand, axis, 0, 0, axis_index_groups=groups, tiled=True)


def swap_cores(block):
    return lax.ppermute(block, "rows", [(i, i ^ 1) for i in range(lax.axis_size("rows"))])


def shift(block, axis, distance):
    count = lax.axis_size(axis)
    route = [(i, i + distance) for i in range(count) if 0 <= i + distance < count]
    return lax.ppermute(block, axis, route)


def along_x(block):
    count = lax.axis_size("tm")
    routes = [[(i, i ^ (mask * 16)) for i in range(count)] for mask in (1, 2, 3)]
    return [block] + [lax.ppermute(block, "tm", route) for route in routes]


def beyond_chip(block):
    count = lax.axis_size("rows")
    route = [(i - 1, i) for i in range(2, count, 2)] + [(i + 1, i) for i in range(1, count - 1, 2)]
    return lax.ppermute(block, "rows", route)


def after(value, *others):
    return lax.optimization_barrier((value,) + others)[0]


def fill_shifts(out, piece, frames, at):
    count, rows = piece.shape[:2]
    flat = piece.reshape(count * rows * W, piece.shape[3]).astype(F32)
    column = lax.broadcasted_iota(jnp.int32, flat.shape, 0) % W
    before = jnp.where(column == 0, 0.0, pltpu.roll(flat, 1, 0))
    behind = jnp.where(column == W - 1, 0.0, pltpu.roll(flat, flat.shape[0] - 1, 0))
    out[1, frames, pl.ds(at, rows)] = piece
    out[0, frames, pl.ds(at, rows)] = before.astype(BF).reshape(piece.shape)
    out[2, frames, pl.ds(at, rows)] = behind.astype(BF).reshape(piece.shape)


def normalize(pre, squares, gain):
    scale = lax.rsqrt(squares * (1.0 / C) + EPS)
    normed = pre * scale
    gated = normed * gain
    sigma = 1.0 / (1.0 + jnp.exp(-gated))
    return scale, normed, gated, sigma


def fill_all(out, flags, field, base, count, far, channels=C):
    mid, edge, other = field
    core = flags[2]
    for f in range(0, count, 2):
        frames = slice(f, f + 2)
        source = slice(base + f, base + f + 2)
        fill_shifts(out, mid[source, :, :, :channels], frames, 3)
        fill_shifts(out, edge[source, :, :, :channels], frames, 1 + 4 * core)
        fill_shifts(out, other[source, :2, :, :channels], frames, 5 - 4 * core)
        if far:
            fill_shifts(out, other[source, 2:, :, :channels], frames, 0)
            for k in range(3):
                out[k, frames, 7:8] = out[k, frames, 0:1]


def place(flags, mask):
    return pl.ds(pl.multiple_of(flags[5 + mask] * 1728, 64), 1728)


def assemble_kernel(flags, a, b, c, d, out):
    for mask, block in enumerate((a, b, c, d)):
        out[place(flags, mask)] = block[...]


def gains_kernel(flags, gain, half, both):
    row = lax.broadcasted_iota(jnp.int32, (C, HALF), 0)
    col = lax.broadcasted_iota(jnp.int32, (C, HALF), 1)
    wide = jnp.broadcast_to(gain[...], (HALF, C)).T
    even = jnp.sum(jnp.where(row == 2 * col, wide, 0.0), axis=0, keepdims=True)
    odd = jnp.sum(jnp.where(row == 2 * col + 1, wide, 0.0), axis=0, keepdims=True)
    half[...] = jnp.where(flags[2] == 0, even, odd)
    both[...] = jnp.concatenate([even, odd], axis=1)


def unpack_kernel(block, out):
    rows = [block[n].astype(F32) for n in range(16)]
    out[...] = jnp.concatenate(rows, axis=0).astype(BF)


def half_kernel(flags, mid, edge, other, w1, pre, squares, xs):
    base = 2 - 2 * flags[2]
    fill_all(xs, flags, (mid, edge, other), 0, 6, True)
    for i in range(3):
        for j in range(3):
            lhs = jnp.concatenate(
                [xs[k, i : i + 4, pl.ds(base + j, 4)].reshape(512, C) for k in range(3)], axis=1
            )
            at = (i * 3 + j) * 3 * C
            part = jnp.dot(lhs, w1[at : at + 3 * C], preferred_element_type=F32)
            if i == 0 and j == 0:
                pre[...] = part
            else:
                pre[...] += part
    total = jnp.sum(pre[...] * pre[...], axis=1, keepdims=True)
    squares[...] = jnp.broadcast_to(total, (512, HALF))


def terms_kernel(flags, pre, own, others, gain, mid, edge, other, out, cs):
    base = 2 - 2 * flags[2]
    fill_all(cs, flags, (mid, edge, other), 8, 6, True, CH)
    _, _, gated, sigma = normalize(pre[...], own[...] + others[...], gain[...])
    act = (gated * sigma).T.astype(BF)
    taps = [(i, j, k) for i in range(3) for j in range(3) for k in range(3)]

    def operand(i, j, k):
        return cs[2 - k, 2 - i : 6 - i, pl.ds(base + 2 - j, 4)].reshape(512, CH)

    for n in range(0, 27, 2):
        pair = taps[n : n + 2]
        rhs = jnp.concatenate([operand(*tap) for tap in pair], axis=1)
        term = jnp.dot(act, rhs, preferred_element_type=F32).astype(BF)
        for m in range(len(pair)):
            out[(n + m) * HALF : (n + m + 1) * HALF] = term[:, m * CH : (m + 1) * CH]


def halves_in_order(flags, value):
    turned = jnp.concatenate([value[..., HALF:], value[..., :HALF]], axis=-1)
    return jnp.where(flags[2] == 1, turned, value)


def pre_kernel(flags, mid, edge, others, own, other, pre, acc, xs):
    fill_all(xs, flags, (mid, edge, others), 0, 8, False)
    for i in range(3):
        for j in range(3):
            lhs = jnp.concatenate(
                [xs[k, i : i + 6, j + 1 : j + 5].reshape(768, C) for k in range(3)], axis=1
            )
            at = (i * 3 + j) * 3 * C
            rhs = jnp.concatenate([own[at : at + 3 * C], other[at : at + 3 * C]], axis=1)
            part = jnp.dot(lhs, rhs, preferred_element_type=F32)
            if i == 0 and j == 0:
                acc[...] = part
            else:
                acc[...] += part
    pre[...] = halves_in_order(flags, acc[...])


def backward_kernel(
    flags, mid, edge, other, gain, pre, w1_own, w1_other, a, b, c, d, far_a, far_b, far_c, far_d,
    out, ps, acc, cs, w2_own, w2_other,
):
    fill_all(cs, flags, (mid, edge, other), 8, 8, False)
    assemble_kernel(flags, a, b, c, d, w2_own)
    assemble_kernel(flags, far_a, far_b, far_c, far_d, w2_other)
    nt = (((1,), (1,)), ((), ()))
    taps = [(i, j, k) for i in range(3) for j in range(3) for k in range(3)]
    for n, (i, j, k) in enumerate(taps):
        lhs = halves_in_order(flags, cs[2 - k, 2 - i : 8 - i, 3 - j : 7 - j].reshape(768, C))
        at = n * C
        rhs = jnp.concatenate([w2_own[at : at + C], w2_other[at : at + C]], axis=1)
        part = lax.dot_general(lhs, rhs, nt, preferred_element_type=F32)
        if n == 0:
            acc[...] = part
        else:
            acc[...] += part
    row = lax.broadcasted_iota(jnp.int32, (C, C), 0)
    col = lax.broadcasted_iota(jnp.int32, (C, C), 1)
    source = jnp.where(col < HALF, 2 * col, 2 * (col - HALF) + 1)
    permutation = jnp.where(row == source, 1.0, 0.0).astype(BF)
    for t in range(6):
        natural = acc[t * 128 : t * 128 + 128]
        high = natural.astype(BF)
        rest = natural - high.astype(F32)
        middle = rest.astype(BF)
        low = (rest - middle.astype(F32)).astype(BF)
        moved = [
            jnp.dot(piece, permutation, preferred_element_type=F32) for piece in (high, middle, low)
        ]
        act_grad = (moved[0] + moved[1]) + moved[2]
        here = pre[t * 128 : t * 128 + 128]
        squares = jnp.sum(here * here, axis=-1, keepdims=True)
        scale, normed, gated, sigma = normalize(here, squares, gain[...])
        norm_grad = act_grad * sigma * (1.0 + gated * (1.0 - sigma)) * gain[...]
        pre_grad = scale * (
            norm_grad - normed * jnp.mean(norm_grad * normed, axis=-1, keepdims=True)
        )
        line = lax.broadcasted_iota(jnp.int32, pre_grad.shape, 0) // W
        outside = ((line == 0) & (flags[1] == 0)) | ((line == 3) & (flags[1] == flags[4]))
        if t >= 4:
            outside = outside | (flags[0] == flags[3])
        pre_grad = jnp.where(outside, 0.0, pre_grad)
        pre_grad = halves_in_order(flags, pre_grad).astype(BF).reshape(1, 4, W, C)
        fill_shifts(ps, pre_grad, slice(t, t + 1), 0)
    for n, (i, j, k) in enumerate(taps):
        lhs = ps[2 - k, 2 - i : 6 - i, 2 - j : 4 - j].reshape(256, C)
        at = n * C
        rhs = jnp.concatenate([w1_own[at : at + C], w1_other[at : at + C]], axis=1)
        part = lax.dot_general(lhs, rhs, nt, preferred_element_type=F32)
        if n == 0:
            acc[:256] = part
        else:
            acc[:256] += part
    out[...] = acc[:256].reshape(4, 2, W, C).astype(BF)


VMEM = pl.BlockSpec(memory_space=pltpu.VMEM)
SMEM = pl.BlockSpec(memory_space=pltpu.SMEM)


def call(kernel, name, flops, out_shape, scratch, *operands):
    smem = [SMEM] if operands[0].dtype == jnp.int32 else []
    return pl.pallas_call(
        kernel,
        out_shape=out_shape,
        in_specs=smem + [VMEM] * (len(operands) - len(smem)),
        out_specs=jax.tree.map(lambda _: VMEM, out_shape),
        scratch_shapes=scratch,
        compiler_params=pltpu.CompilerParams(vmem_limit_bytes=24 * 1024 * 1024),
        cost_estimate=pl.CostEstimate(flops=flops, bytes_accessed=1 << 20, transcendentals=0),
        name=name,
    )(*operands)


def order_gains(flags, gain):
    half = jax.ShapeDtypeStruct((1, HALF), F32)
    both = jax.ShapeDtypeStruct((1, C), F32)
    return call(gains_kernel, "gains", GAINS_COST, (half, both), [], flags, gain.reshape(1, C))


def unpack(block, cost=1):
    shape = jax.ShapeDtypeStruct((1728, HALF), BF)
    return call(unpack_kernel, "unpack", cost, shape, [], block)


def assemble(flags, blocks, cost=1):
    shape = jax.ShapeDtypeStruct((ROWS, HALF), BF)
    return call(assemble_kernel, "assemble", cost, shape, [], flags, *blocks)


def forward_half(flags, field, w1):
    shape = jax.ShapeDtypeStruct((512, HALF), F32)
    scratch = [pltpu.VMEM((3, 6, 8, W, C), BF)]
    return call(
        half_kernel, "forward_half", 4 * 512 * ROWS * HALF, (shape, shape), scratch,
        flags, *field, w1,
    )


def local_terms(flags, pre, own, others, gain, field):
    shape = jax.ShapeDtypeStruct((ROWS // 2, CH), BF)
    scratch = [pltpu.VMEM((3, 6, 8, W, CH), BF)]
    return call(
        terms_kernel, "local_terms", 4 * 512 * ROWS * HALF, shape, scratch,
        flags, pre, own, others, gain, *field,
    )


def forward_all(flags, field, own, other):
    shape = jax.ShapeDtypeStruct((768, C), F32)
    scratch = [pltpu.VMEM((768, C), F32), pltpu.VMEM((3, 8, 8, W, C), BF)]
    return call(
        pre_kernel, "forward_all", 2 * 768 * ROWS * C, shape, scratch, flags, *field, own, other
    )


def backward(flags, field, gain, pre, w1_own, w1_other, w2_own, w2_other):
    shape = jax.ShapeDtypeStruct((4, 2, W, C), BF)
    scratch = [
        pltpu.VMEM((3, 6, 4, W, C), BF),
        pltpu.VMEM((768, C), F32),
        pltpu.VMEM((3, 8, 8, W, C), BF),
        pltpu.VMEM((ROWS, HALF), BF),
        pltpu.VMEM((ROWS, HALF), BF),
    ]
    return call(
        backward_kernel, "backward", 2 * 1024 * ROWS * C, shape, scratch,
        flags, *field, gain, pre, w1_own, w1_other, *w2_own, *w2_other,
    )


def on_device(activations, cotangent, gain, first_weight, second_weight):
    tm, rows = lax.axis_index("tm"), lax.axis_index("rows")
    core, x = rows % 2, tm // 16
    flags = [tm, rows, core, lax.axis_size("tm") - 1, lax.axis_size("rows") - 1]
    flags = jnp.stack(flags + [x ^ mask for mask in range(4)]).astype(jnp.int32)

    pick = lax.broadcasted_iota(jnp.int32, (C, HALF), 0) == (
        2 * lax.broadcasted_iota(jnp.int32, (C, HALF), 1) + core
    )
    half1 = jnp.dot(first_weight, pick.astype(BF), preferred_element_type=F32).astype(BF)
    half2 = lax.dynamic_slice_in_dim(second_weight, core * HALF, HALF, axis=1)

    operand = jnp.broadcast_to(half1[None], (16,) + half1.shape)
    w1_block = lax.all_to_all(operand, "tm", 0, 0, axis_index_groups=YZ_GROUPS, tiled=True)
    w1_blocks = along_x(unpack(w1_block, UNPACK_COST))
    activations, cotangent, _ = lax.optimization_barrier((activations, cotangent, operand))

    nexts = shift(jnp.concatenate([activations[:2], cotangent], axis=0), "tm", -1)
    prevs = shift(activations[2:], "tm", 1)
    gain_half, gain_all = order_gains(flags, gain)
    nexts, prevs = lax.optimization_barrier((nexts, prevs, gain_half))[:2]
    mid = jnp.concatenate([prevs, activations, nexts[:2], cotangent, nexts[2:]], axis=0)
    edge = beyond_chip(mid)
    next_row = jnp.where(core == 0, edge[:, 1:], edge[:, :1])
    field = (mid, edge, swap_cores(jnp.concatenate([mid, next_row], axis=1)))

    w2_block = unpack(spread(after(half2, edge), "tm", YZ_GROUPS))

    w1_own = assemble(flags, w1_blocks, ASSEMBLE_COST)
    pre_half, squares = forward_half(flags, field, w1_own)
    squares_other = swap_cores(squares)
    squares_other, w2_block = lax.optimization_barrier((squares_other, w2_block))
    terms = local_terms(flags, pre_half, squares, squares_other, gain_half, field)

    total = lax.all_to_all(
        terms.reshape(4, 864, CH), "tm", 0, 0, axis_index_groups=X_GROUPS, tiled=True
    )
    w1_other = swap_cores(after(w1_own, terms))
    w2_blocks = along_x(after(w2_block, terms))
    pre = forward_all(flags, field, w1_own, w1_other)
    total, pre = lax.optimization_barrier((total, pre))

    total = total.astype(F32).sum(0).astype(BF).reshape(16, 54, CH)
    total = lax.all_to_all(total, "tm", 0, 0, axis_index_groups=YZ_GROUPS, tiled=True)
    w2_far = [swap_cores(block) for block in w2_blocks]
    input_grad = backward(flags, field, gain_all, pre, w1_own, w1_other, w2_blocks, w2_far)
    total = spread(total.astype(F32).sum(0), "rows", ROW_GROUPS)
    total, input_grad = lax.optimization_barrier((total, input_grad))
    weight_grad = total.reshape(4, 2, 54, CH).sum(0).transpose(1, 0, 2).reshape(108, CH)
    return (input_grad, weight_grad)


def solution(mesh):
    return jax.shard_map(
        on_device,
        mesh=mesh,
        in_specs=(
            P("tm", "rows", None, None),
            P("tm", "rows", None, None),
            P(),
            P("tm", None),
            P("tm", None),
        ),
        out_specs=(P("tm", "rows", None, None), P("tm", None)),
        check_vma=False,
    )
```

```python
import jax
import jax.numpy as jnp
from jax import lax
from jax.experimental import pallas as pl
from jax.experimental.pallas import tpu as pltpu
from jax.sharding import PartitionSpec as P

CH = 128
C = 256
W = 32
HALF = 128
ROWS = 6912
EPS = 1e-06
BF = jnp.bfloat16
F32 = jnp.float32

YZ_GROUPS = [[x * 16 + k for k in range(16)] for x in range(4)]
X_GROUPS = [[k, k + 16, k + 32, k + 48] for k in range(16)]
ROW_GROUPS = [list(range(8))]
GAINS_COST = 1 << 36
UNPACK_COST = 1 << 36
GATE_COST = 1 << 36


def spread(block, axis, groups):
    count = len(groups[0])
    operand = jnp.broadcast_to(block[None], (count,) + block.shape)
    return lax.all_to_all(operand, axis, 0, 0, axis_index_groups=groups, tiled=True)


def swap_cores(block):
    return lax.ppermute(block, "rows", [(i, i ^ 1) for i in range(lax.axis_size("rows"))])


def shift(block, axis, distance):
    count = lax.axis_size(axis)
    route = [(i, i + distance) for i in range(count) if 0 <= i + distance < count]
    return lax.ppermute(block, axis, route)


def along_x(block):
    count = lax.axis_size("tm")
    routes = [[(i, i ^ (mask * 16)) for i in range(count)] for mask in (1, 3, 2)]
    return [block] + [lax.ppermute(block, "tm", route) for route in routes]


def beyond_chip(block):
    count = lax.axis_size("rows")
    route = [(i - 1, i) for i in range(2, count, 2)] + [(i + 1, i) for i in range(1, count - 1, 2)]
    return lax.ppermute(block, "rows", route)


def after(value, *others):
    return lax.optimization_barrier((value,) + others)[0]


def fill_shifts(out, piece, frames, at):
    count, rows = piece.shape[:2]
    flat = piece.reshape(count * rows * W, piece.shape[3]).astype(F32)
    column = lax.broadcasted_iota(jnp.int32, flat.shape, 0) % W
    before = jnp.where(column == 0, 0.0, pltpu.roll(flat, 1, 0))
    behind = jnp.where(column == W - 1, 0.0, pltpu.roll(flat, flat.shape[0] - 1, 0))
    out[1, frames, pl.ds(at, rows)] = piece
    out[0, frames, pl.ds(at, rows)] = before.astype(BF).reshape(piece.shape)
    out[2, frames, pl.ds(at, rows)] = behind.astype(BF).reshape(piece.shape)


def normalize(pre, squares, gain):
    scale = lax.rsqrt(squares * (1.0 / C) + EPS)
    normed = pre * scale
    gated = normed * gain
    sigma = 1.0 / (1.0 + jnp.exp(-gated))
    return scale, normed, gated, sigma


def fill_all(out, flags, field, base, count, far, channels=C):
    mid, edge, other = field
    core = flags[2]
    for f in range(0, count, 2):
        frames = slice(f, f + 2)
        source = slice(base + f, base + f + 2)
        fill_shifts(out, mid[source, :, :, :channels], frames, 3)
        fill_shifts(out, edge[source, :, :, :channels], frames, 1 + 4 * core)
        fill_shifts(out, other[source, :2, :, :channels], frames, 5 - 4 * core)
        if far:
            fill_shifts(out, other[source, 2:, :, :channels], frames, 0)
            for k in range(3):
                out[k, frames, 7:8] = out[k, frames, 0:1]


def place(flags, n):
    return pl.ds(pl.multiple_of(flags[5 + n] * 1728, 64), 1728)


def assemble_kernel(flags, a, b, c, d, out):
    for n, block in enumerate((a, b, c, d)):
        out[place(flags, n)] = block[...]


def gains_kernel(flags, gain, half, both):
    row = lax.broadcasted_iota(jnp.int32, (C, HALF), 0)
    col = lax.broadcasted_iota(jnp.int32, (C, HALF), 1)
    wide = jnp.broadcast_to(gain[...], (HALF, C)).T
    even = jnp.sum(jnp.where(row == 2 * col, wide, 0.0), axis=0, keepdims=True)
    odd = jnp.sum(jnp.where(row == 2 * col + 1, wide, 0.0), axis=0, keepdims=True)
    half[...] = jnp.where(flags[2] == 0, even, odd)
    both[...] = jnp.concatenate([even, odd], axis=1)


def unpack_kernel(block, out):
    rows = [block[n].astype(F32) for n in range(16)]
    out[...] = jnp.concatenate(rows, axis=0).astype(BF)


def half_kernel(flags, mid, edge, other, a, b, c, d, pre, squares, w1, xs):
    base = 2 - 2 * flags[2]
    fill_all(xs, flags, (mid, edge, other), 0, 6, True)
    assemble_kernel(flags, a, b, c, d, w1)
    for i in range(3):
        for j in range(3):
            lhs = jnp.concatenate(
                [xs[k, i : i + 4, pl.ds(base + j, 4)].reshape(512, C) for k in range(3)], axis=1
            )
            at = (i * 3 + j) * 3 * C
            part = jnp.dot(lhs, w1[at : at + 3 * C], preferred_element_type=F32)
            if i == 0 and j == 0:
                pre[...] = part
            else:
                pre[...] += part
    total = jnp.sum(pre[...] * pre[...], axis=1, keepdims=True)
    squares[...] = jnp.broadcast_to(total, (512, HALF))


def terms_kernel(flags, pre, own, others, gain, mid, edge, other, out, cs):
    base = 2 - 2 * flags[2]
    fill_all(cs, flags, (mid, edge, other), 8, 6, True, CH)
    _, _, gated, sigma = normalize(pre[...], own[...] + others[...], gain[...])
    act = (gated * sigma).T.astype(BF)
    taps = [(i, j, k) for i in range(3) for j in range(3) for k in range(3)]

    def operand(i, j, k):
        return cs[2 - k, 2 - i : 6 - i, pl.ds(base + 2 - j, 4)].reshape(512, CH)

    for n in range(0, 27, 2):
        pair = taps[n : n + 2]
        rhs = jnp.concatenate([operand(*tap) for tap in pair], axis=1)
        term = jnp.dot(act, rhs, preferred_element_type=F32).astype(BF)
        for m in range(len(pair)):
            out[(n + m) * HALF : (n + m + 1) * HALF] = term[:, m * CH : (m + 1) * CH]


def halves_in_order(flags, value):
    turned = jnp.concatenate([value[..., HALF:], value[..., :HALF]], axis=-1)
    return jnp.where(flags[2] == 1, turned, value)


def pre_kernel(flags, mid, edge, others, own, other, pre, acc, xs):
    fill_all(xs, flags, (mid, edge, others), 0, 8, False)
    for i in range(3):
        for j in range(3):
            lhs = jnp.concatenate(
                [xs[k, i : i + 6, j + 1 : j + 5].reshape(768, C) for k in range(3)], axis=1
            )
            at = (i * 3 + j) * 3 * C
            rhs = jnp.concatenate([own[at : at + 3 * C], other[at : at + 3 * C]], axis=1)
            part = jnp.dot(lhs, rhs, preferred_element_type=F32)
            if i == 0 and j == 0:
                acc[...] = part
            else:
                acc[...] += part
    pre[...] = halves_in_order(flags, acc[...])


def backward_kernel(
    flags, mid, edge, other, gain, pre, own_in, other_in, a, b, c, d, far_a, far_b, far_c, far_d,
    out, ps, acc, cs, w2_own, w2_other, w1_own, w1_other, sems,
):
    pairs = ((own_in, w1_own), (other_in, w1_other))
    copies = [pltpu.make_async_copy(source, to, sems.at[n]) for n, (source, to) in enumerate(pairs)]
    for copy in copies:
        copy.start()
    fill_all(cs, flags, (mid, edge, other), 8, 8, False)
    assemble_kernel(flags, a, b, c, d, w2_own)
    assemble_kernel(flags, far_a, far_b, far_c, far_d, w2_other)
    nt = (((1,), (1,)), ((), ()))
    taps = [(i, j, k) for i in range(3) for j in range(3) for k in range(3)]
    for n, (i, j, k) in enumerate(taps):
        lhs = halves_in_order(flags, cs[2 - k, 2 - i : 8 - i, 3 - j : 7 - j].reshape(768, C))
        at = n * C
        rhs = jnp.concatenate([w2_own[at : at + C], w2_other[at : at + C]], axis=1)
        part = lax.dot_general(lhs, rhs, nt, preferred_element_type=F32)
        if n == 0:
            acc[...] = part
        else:
            acc[...] += part
    row = lax.broadcasted_iota(jnp.int32, (C, C), 0)
    col = lax.broadcasted_iota(jnp.int32, (C, C), 1)
    source = jnp.where(col < HALF, 2 * col, 2 * (col - HALF) + 1)
    permutation = jnp.where(row == source, 1.0, 0.0).astype(BF)
    for t in range(6):
        natural = acc[t * 128 : t * 128 + 128]
        high = natural.astype(BF)
        rest = natural - high.astype(F32)
        middle = rest.astype(BF)
        low = (rest - middle.astype(F32)).astype(BF)
        moved = [
            jnp.dot(piece, permutation, preferred_element_type=F32) for piece in (high, middle, low)
        ]
        act_grad = (moved[0] + moved[1]) + moved[2]
        here = pre[t * 128 : t * 128 + 128]
        squares = jnp.sum(here * here, axis=-1, keepdims=True)
        scale, normed, gated, sigma = normalize(here, squares, gain[...])
        norm_grad = act_grad * sigma * (1.0 + gated * (1.0 - sigma)) * gain[...]
        pre_grad = scale * (
            norm_grad - normed * jnp.mean(norm_grad * normed, axis=-1, keepdims=True)
        )
        line = lax.broadcasted_iota(jnp.int32, pre_grad.shape, 0) // W
        outside = ((line == 0) & (flags[1] == 0)) | ((line == 3) & (flags[1] == flags[4]))
        if t >= 4:
            outside = outside | (flags[0] == flags[3])
        pre_grad = jnp.where(outside, 0.0, pre_grad)
        pre_grad = halves_in_order(flags, pre_grad).astype(BF).reshape(1, 4, W, C)
        fill_shifts(ps, pre_grad, slice(t, t + 1), 0)
    for copy in copies:
        copy.wait()
    for n, (i, j, k) in enumerate(taps):
        lhs = ps[2 - k, 2 - i : 6 - i, 2 - j : 4 - j].reshape(256, C)
        at = n * C
        rhs = jnp.concatenate([w1_own[at : at + C], w1_other[at : at + C]], axis=1)
        part = lax.dot_general(lhs, rhs, nt, preferred_element_type=F32)
        if n == 0:
            acc[:256] = part
        else:
            acc[:256] += part
    out[...] = acc[:256].reshape(4, 2, W, C).astype(BF)


VMEM = pl.BlockSpec(memory_space=pltpu.VMEM)
SMEM = pl.BlockSpec(memory_space=pltpu.SMEM)


def call(kernel, name, flops, out_shape, scratch, *operands):
    smem = [SMEM] if operands[0].dtype == jnp.int32 else []
    return pl.pallas_call(
        kernel,
        out_shape=out_shape,
        in_specs=smem + [VMEM] * (len(operands) - len(smem)),
        out_specs=jax.tree.map(lambda _: VMEM, out_shape),
        scratch_shapes=scratch,
        compiler_params=pltpu.CompilerParams(vmem_limit_bytes=24 * 1024 * 1024),
        cost_estimate=pl.CostEstimate(flops=flops, bytes_accessed=1 << 20, transcendentals=0),
        name=name,
    )(*operands)


def order_gains(flags, gain):
    half = jax.ShapeDtypeStruct((1, HALF), F32)
    both = jax.ShapeDtypeStruct((1, C), F32)
    return call(gains_kernel, "gains", GAINS_COST, (half, both), [], flags, gain.reshape(1, C))


def unpack(block, cost=1):
    shape = jax.ShapeDtypeStruct((1728, HALF), BF)
    return call(unpack_kernel, "unpack", cost, shape, [], block)


def gate_kernel(flags, out):
    for n in range(9):
        out[n] = flags[n]


def gate(flags):
    return pl.pallas_call(
        gate_kernel,
        out_shape=jax.ShapeDtypeStruct((9,), jnp.int32),
        in_specs=[SMEM],
        out_specs=SMEM,
        cost_estimate=pl.CostEstimate(flops=GATE_COST, bytes_accessed=1, transcendentals=0),
        name="gate",
    )(flags)


def forward_half(flags, field, blocks):
    shape = jax.ShapeDtypeStruct((512, HALF), F32)
    weight = jax.ShapeDtypeStruct((ROWS, HALF), BF)
    scratch = [pltpu.VMEM((3, 6, 8, W, C), BF)]
    return call(
        half_kernel, "forward_half", 4 * 512 * ROWS * HALF, (shape, shape, weight), scratch,
        flags, *field, *blocks,
    )


def local_terms(flags, pre, own, others, gain, field):
    shape = jax.ShapeDtypeStruct((ROWS // 2, CH), BF)
    scratch = [pltpu.VMEM((3, 6, 8, W, CH), BF)]
    return call(
        terms_kernel, "local_terms", 4 * 512 * ROWS * HALF, shape, scratch,
        flags, pre, own, others, gain, *field,
    )


def forward_all(flags, field, own, other):
    shape = jax.ShapeDtypeStruct((768, C), F32)
    scratch = [pltpu.VMEM((768, C), F32), pltpu.VMEM((3, 8, 8, W, C), BF)]
    return call(
        pre_kernel, "forward_all", 2 * 768 * ROWS * C, shape, scratch, flags, *field, own, other
    )


def backward(flags, field, gain, pre, w1_own, w1_other, w2_own, w2_other):
    weight = pltpu.VMEM((ROWS, HALF), BF)
    kept = pl.BlockSpec(memory_space=pl.ANY)
    return pl.pallas_call(
        backward_kernel,
        out_shape=jax.ShapeDtypeStruct((4, 2, W, C), BF),
        in_specs=[SMEM] + [VMEM] * 5 + [kept] * 2 + [VMEM] * 8,
        out_specs=VMEM,
        scratch_shapes=[
            pltpu.VMEM((3, 6, 4, W, C), BF),
            pltpu.VMEM((768, C), F32),
            pltpu.VMEM((3, 8, 8, W, C), BF),
            weight,
            weight,
            weight,
            weight,
            pltpu.SemaphoreType.DMA((2,)),
        ],
        compiler_params=pltpu.CompilerParams(vmem_limit_bytes=32 * 1024 * 1024),
        cost_estimate=pl.CostEstimate(
            flops=2 * 1024 * ROWS * C, bytes_accessed=10 << 20, transcendentals=0
        ),
        name="backward",
    )(flags, *field, gain, pre, w1_own, w1_other, *w2_own, *w2_other)


def on_device(activations, cotangent, gain, first_weight, second_weight):
    tm, rows = lax.axis_index("tm"), lax.axis_index("rows")
    core, x = rows % 2, tm // 16
    flags = [tm, rows, core, lax.axis_size("tm") - 1, lax.axis_size("rows") - 1]
    flags = jnp.stack(flags + [x ^ mask for mask in (0, 1, 3, 2)]).astype(jnp.int32)

    pick = lax.broadcasted_iota(jnp.int32, (C, HALF), 0) == (
        2 * lax.broadcasted_iota(jnp.int32, (C, HALF), 1) + core
    )
    half1 = jnp.dot(first_weight, pick.astype(BF), preferred_element_type=F32).astype(BF)
    half2 = lax.dynamic_slice_in_dim(second_weight, core * HALF, HALF, axis=1)

    operand = jnp.broadcast_to(half1[None], (16,) + half1.shape)
    w1_block = lax.all_to_all(operand, "tm", 0, 0, axis_index_groups=YZ_GROUPS, tiled=True)
    w1_blocks = along_x(unpack(w1_block, UNPACK_COST))
    activations, cotangent, _ = lax.optimization_barrier((activations, cotangent, operand))

    nexts = shift(jnp.concatenate([activations[:2], cotangent], axis=0), "tm", -1)
    prevs = shift(activations[2:], "tm", 1)
    gain_half, gain_all = order_gains(flags, gain)
    nexts, prevs = lax.optimization_barrier((nexts, prevs, gain_half))[:2]
    mid = jnp.concatenate([prevs, activations, nexts[:2], cotangent, nexts[2:]], axis=0)
    edge = beyond_chip(mid)
    next_row = jnp.where(core == 0, edge[:, 1:], edge[:, :1])
    field = (mid, edge, swap_cores(jnp.concatenate([mid, next_row], axis=1)))

    w2_block = unpack(spread(after(half2, edge), "tm", YZ_GROUPS))

    behind = gate(after(flags, *w1_blocks))
    pre_half, squares, w1_own = forward_half(behind, field, w1_blocks)
    squares_other = swap_cores(squares)
    squares_other, w2_block = lax.optimization_barrier((squares_other, w2_block))
    terms = local_terms(flags, pre_half, squares, squares_other, gain_half, field)

    total = lax.all_to_all(
        terms.reshape(4, 864, CH), "tm", 0, 0, axis_index_groups=X_GROUPS, tiled=True
    )
    w1_other = swap_cores(after(w1_own, terms))
    w2_blocks = along_x(after(w2_block, terms))
    pre = forward_all(flags, field, w1_own, w1_other)
    total, pre = lax.optimization_barrier((total, pre))

    total = total.astype(F32).sum(0).astype(BF).reshape(16, 54, CH)
    total = lax.all_to_all(total, "tm", 0, 0, axis_index_groups=YZ_GROUPS, tiled=True)
    w2_far = [swap_cores(block) for block in w2_blocks]
    input_grad = backward(flags, field, gain_all, pre, w1_own, w1_other, w2_blocks, w2_far)
    total = spread(total.astype(F32).sum(0), "rows", ROW_GROUPS)
    total, input_grad = lax.optimization_barrier((total, input_grad))
    weight_grad = total.reshape(4, 2, 54, CH).sum(0).transpose(1, 0, 2).reshape(108, CH)
    return (input_grad, weight_grad)


def solution(mesh):
    return jax.shard_map(
        on_device,
        mesh=mesh,
        in_specs=(
            P("tm", "rows", None, None),
            P("tm", "rows", None, None),
            P(),
            P("tm", None),
            P("tm", None),
        ),
        out_specs=(P("tm", "rows", None, None), P("tm", None)),
        check_vma=False,
    )
```

```python
import jax
import jax.numpy as jnp
from jax import lax
from jax.experimental import pallas as pl
from jax.experimental.pallas import tpu as pltpu
from jax.sharding import PartitionSpec as P

CH = 128
C = 256
W = 32
HALF = 128
ROWS = 6912
EPS = 1e-06
BF = jnp.bfloat16
F32 = jnp.float32

YZ_GROUPS = [[x * 16 + k for k in range(16)] for x in range(4)]
X_GROUPS = [[k, k + 16, k + 32, k + 48] for k in range(16)]
ROW_GROUPS = [list(range(8))]
GAINS_COST = 1 << 36
UNPACK_COST = 1 << 36
GATE_COST = 1 << 36


def spread(block, axis, groups):
    count = len(groups[0])
    operand = jnp.broadcast_to(block[None], (count,) + block.shape)
    return lax.all_to_all(operand, axis, 0, 0, axis_index_groups=groups, tiled=True)


def swap_cores(block):
    return lax.ppermute(block, "rows", [(i, i ^ 1) for i in range(lax.axis_size("rows"))])


def shift(block, axis, distance):
    count = lax.axis_size(axis)
    route = [(i, i + distance) for i in range(count) if 0 <= i + distance < count]
    return lax.ppermute(block, axis, route)


def along_x(block):
    count = lax.axis_size("tm")
    routes = [[(i, i ^ (mask * 16)) for i in range(count)] for mask in (1, 3, 2)]
    return [block] + [lax.ppermute(block, "tm", route) for route in routes]


def beyond_chip(block):
    count = lax.axis_size("rows")
    route = [(i - 1, i) for i in range(2, count, 2)] + [(i + 1, i) for i in range(1, count - 1, 2)]
    return lax.ppermute(block, "rows", route)


def after(value, *others):
    return lax.optimization_barrier((value,) + others)[0]


def fill_shifts(out, piece, frames, at):
    count, rows = piece.shape[:2]
    flat = piece.reshape(count * rows * W, piece.shape[3]).astype(F32)
    column = lax.broadcasted_iota(jnp.int32, flat.shape, 0) % W
    before = jnp.where(column == 0, 0.0, pltpu.roll(flat, 1, 0))
    behind = jnp.where(column == W - 1, 0.0, pltpu.roll(flat, flat.shape[0] - 1, 0))
    out[1, frames, pl.ds(at, rows)] = piece
    out[0, frames, pl.ds(at, rows)] = before.astype(BF).reshape(piece.shape)
    out[2, frames, pl.ds(at, rows)] = behind.astype(BF).reshape(piece.shape)


def normalize(pre, squares, gain):
    scale = lax.rsqrt(squares * (1.0 / C) + EPS)
    normed = pre * scale
    gated = normed * gain
    sigma = 1.0 / (1.0 + jnp.exp(-gated))
    return scale, normed, gated, sigma


def fill_all(out, flags, field, base, count, far, channels=C):
    mid, edge, other = field
    core = flags[2]
    for f in range(0, count, 2):
        frames = slice(f, f + 2)
        source = slice(base + f, base + f + 2)
        fill_shifts(out, mid[source, :, :, :channels], frames, 3)
        fill_shifts(out, edge[source, :, :, :channels], frames, 1 + 4 * core)
        fill_shifts(out, other[source, :2, :, :channels], frames, 5 - 4 * core)
        if far:
            fill_shifts(out, other[source, 2:, :, :channels], frames, 0)
            for k in range(3):
                out[k, frames, 7:8] = out[k, frames, 0:1]


def place(flags, n):
    return pl.ds(pl.multiple_of(flags[5 + n] * 1728, 64), 1728)


def assemble_kernel(flags, a, b, c, d, out):
    for n, block in enumerate((a, b, c, d)):
        out[place(flags, n)] = block[...]


def gains_kernel(flags, gain, half, both):
    row = lax.broadcasted_iota(jnp.int32, (C, HALF), 0)
    col = lax.broadcasted_iota(jnp.int32, (C, HALF), 1)
    wide = jnp.broadcast_to(gain[...], (HALF, C)).T
    even = jnp.sum(jnp.where(row == 2 * col, wide, 0.0), axis=0, keepdims=True)
    odd = jnp.sum(jnp.where(row == 2 * col + 1, wide, 0.0), axis=0, keepdims=True)
    half[...] = jnp.where(flags[2] == 0, even, odd)
    both[...] = jnp.concatenate([even, odd], axis=1)


def unpack_kernel(block, out):
    rows = [block[n].astype(F32) for n in range(16)]
    out[...] = jnp.concatenate(rows, axis=0).astype(BF)


def sum_kernel(terms, out):
    total = terms[0].astype(F32) + terms[1].astype(F32)
    total = (total + terms[2].astype(F32)) + terms[3].astype(F32)
    for n in range(16):
        out[n] = total[n * 54 : n * 54 + 54].astype(BF)


def half_kernel(flags, gated, mid, edge, other, a, b, c, d, pre, squares, w1, xs):
    base = 2 - 2 * flags[2]
    fill_all(xs, flags, (mid, edge, other), 0, 6, True)
    assemble_kernel(flags, a, b, c, d, w1)
    for i in range(3):
        for j in range(3):
            lhs = jnp.concatenate(
                [xs[k, i : i + 4, pl.ds(base + j, 4)].reshape(512, C) for k in range(3)], axis=1
            )
            at = (i * 3 + j) * 3 * C
            part = jnp.dot(lhs, w1[at : at + 3 * C], preferred_element_type=F32)
            if i == 0 and j == 0:
                pre[...] = part
            else:
                pre[...] += part
    total = jnp.sum(pre[...] * pre[...], axis=1, keepdims=True)
    squares[...] = jnp.broadcast_to(total, (512, HALF))


def terms_kernel(flags, pre, own, others, gain, mid, edge, other, out, cs):
    base = 2 - 2 * flags[2]
    fill_all(cs, flags, (mid, edge, other), 8, 6, True, CH)
    _, _, gated, sigma = normalize(pre[...], own[...] + others[...], gain[...])
    act = (gated * sigma).T.astype(BF)
    taps = [(i, j, k) for i in range(3) for j in range(3) for k in range(3)]

    def operand(i, j, k):
        return cs[2 - k, 2 - i : 6 - i, pl.ds(base + 2 - j, 4)].reshape(512, CH)

    for n in range(0, 27, 2):
        pair = taps[n : n + 2]
        rhs = jnp.concatenate([operand(*tap) for tap in pair], axis=1)
        term = jnp.dot(act, rhs, preferred_element_type=F32).astype(BF)
        for m in range(len(pair)):
            out[(n + m) * HALF : (n + m + 1) * HALF] = term[:, m * CH : (m + 1) * CH]


def halves_in_order(flags, value):
    turned = jnp.concatenate([value[..., HALF:], value[..., :HALF]], axis=-1)
    return jnp.where(flags[2] == 1, turned, value)


def pre_kernel(flags, mid, edge, others, own, other, pre, acc, xs):
    fill_all(xs, flags, (mid, edge, others), 0, 8, False)
    for i in range(3):
        for j in range(3):
            lhs = jnp.concatenate(
                [xs[k, i : i + 6, j + 1 : j + 5].reshape(768, C) for k in range(3)], axis=1
            )
            at = (i * 3 + j) * 3 * C
            rhs = jnp.concatenate([own[at : at + 3 * C], other[at : at + 3 * C]], axis=1)
            part = jnp.dot(lhs, rhs, preferred_element_type=F32)
            if i == 0 and j == 0:
                acc[...] = part
            else:
                acc[...] += part
    pre[...] = halves_in_order(flags, acc[...])


def backward_kernel(
    flags, mid, edge, other, gain, pre_in, w1_own, w1_other, a, b, c, d, far_a, far_b, far_c, far_d,
    out, ps, acc, cs, w2_own, w2_other, pre, sem,
):
    copy = pltpu.make_async_copy(pre_in, pre, sem)
    copy.start()
    fill_all(cs, flags, (mid, edge, other), 8, 8, False)
    assemble_kernel(flags, a, b, c, d, w2_own)
    assemble_kernel(flags, far_a, far_b, far_c, far_d, w2_other)
    nt = (((1,), (1,)), ((), ()))
    taps = [(i, j, k) for i in range(3) for j in range(3) for k in range(3)]
    for n, (i, j, k) in enumerate(taps):
        lhs = halves_in_order(flags, cs[2 - k, 2 - i : 8 - i, 3 - j : 7 - j].reshape(768, C))
        at = n * C
        rhs = jnp.concatenate([w2_own[at : at + C], w2_other[at : at + C]], axis=1)
        part = lax.dot_general(lhs, rhs, nt, preferred_element_type=F32)
        if n == 0:
            acc[...] = part
        else:
            acc[...] += part
    copy.wait()
    row = lax.broadcasted_iota(jnp.int32, (C, C), 0)
    col = lax.broadcasted_iota(jnp.int32, (C, C), 1)
    source = jnp.where(col < HALF, 2 * col, 2 * (col - HALF) + 1)
    permutation = jnp.where(row == source, 1.0, 0.0).astype(BF)
    for t in range(6):
        natural = acc[t * 128 : t * 128 + 128]
        high = natural.astype(BF)
        rest = natural - high.astype(F32)
        middle = rest.astype(BF)
        low = (rest - middle.astype(F32)).astype(BF)
        moved = [
            jnp.dot(piece, permutation, preferred_element_type=F32) for piece in (high, middle, low)
        ]
        act_grad = (moved[0] + moved[1]) + moved[2]
        here = pre[t * 128 : t * 128 + 128]
        squares = jnp.sum(here * here, axis=-1, keepdims=True)
        scale, normed, gated, sigma = normalize(here, squares, gain[...])
        norm_grad = act_grad * sigma * (1.0 + gated * (1.0 - sigma)) * gain[...]
        pre_grad = scale * (
            norm_grad - normed * jnp.mean(norm_grad * normed, axis=-1, keepdims=True)
        )
        line = lax.broadcasted_iota(jnp.int32, pre_grad.shape, 0) // W
        outside = ((line == 0) & (flags[1] == 0)) | ((line == 3) & (flags[1] == flags[4]))
        if t >= 4:
            outside = outside | (flags[0] == flags[3])
        pre_grad = jnp.where(outside, 0.0, pre_grad)
        pre_grad = halves_in_order(flags, pre_grad).astype(BF).reshape(1, 4, W, C)
        fill_shifts(ps, pre_grad, slice(t, t + 1), 0)
    for n, (i, j, k) in enumerate(taps):
        lhs = ps[2 - k, 2 - i : 6 - i, 2 - j : 4 - j].reshape(256, C)
        at = n * C
        rhs = jnp.concatenate([w1_own[at : at + C], w1_other[at : at + C]], axis=1)
        part = lax.dot_general(lhs, rhs, nt, preferred_element_type=F32)
        if n == 0:
            acc[:256] = part
        else:
            acc[:256] += part
    out[...] = acc[:256].reshape(4, 2, W, C).astype(BF)


VMEM = pl.BlockSpec(memory_space=pltpu.VMEM)
SMEM = pl.BlockSpec(memory_space=pltpu.SMEM)


def call(kernel, name, flops, out_shape, scratch, *operands):
    smem = [SMEM] if operands[0].dtype == jnp.int32 else []
    return pl.pallas_call(
        kernel,
        out_shape=out_shape,
        in_specs=smem + [VMEM] * (len(operands) - len(smem)),
        out_specs=jax.tree.map(lambda _: VMEM, out_shape),
        scratch_shapes=scratch,
        compiler_params=pltpu.CompilerParams(vmem_limit_bytes=24 * 1024 * 1024),
        cost_estimate=pl.CostEstimate(flops=flops, bytes_accessed=1 << 20, transcendentals=0),
        name=name,
    )(*operands)


def order_gains(flags, gain):
    half = jax.ShapeDtypeStruct((1, HALF), F32)
    both = jax.ShapeDtypeStruct((1, C), F32)
    return call(gains_kernel, "gains", GAINS_COST, (half, both), [], flags, gain.reshape(1, C))


def unpack(block, cost=1):
    shape = jax.ShapeDtypeStruct((1728, HALF), BF)
    return call(unpack_kernel, "unpack", cost, shape, [], block)


def gate_kernel(value, out):
    out[...] = value[...]


def gate(value):
    shape = jax.ShapeDtypeStruct(value.shape, value.dtype)
    return call(gate_kernel, "gate", GATE_COST, shape, [], value)


def sum_terms(terms):
    shape = jax.ShapeDtypeStruct((16, 54, CH), BF)
    return call(sum_kernel, "sum_terms", 1 << 20, shape, [], terms)


def forward_half(flags, gated, field, blocks):
    shape = jax.ShapeDtypeStruct((512, HALF), F32)
    weight = jax.ShapeDtypeStruct((ROWS, HALF), BF)
    scratch = [pltpu.VMEM((3, 6, 8, W, C), BF)]
    return call(
        half_kernel, "forward_half", 4 * 512 * ROWS * HALF, (shape, shape, weight), scratch,
        flags, gated, *field, *blocks,
    )


def local_terms(flags, pre, own, others, gain, field):
    shape = jax.ShapeDtypeStruct((ROWS // 2, CH), BF)
    scratch = [pltpu.VMEM((3, 6, 8, W, CH), BF)]
    return call(
        terms_kernel, "local_terms", 4 * 512 * ROWS * HALF, shape, scratch,
        flags, pre, own, others, gain, *field,
    )


def forward_all(flags, field, own, other):
    shape = jax.ShapeDtypeStruct((768, C), F32)
    scratch = [pltpu.VMEM((768, C), F32), pltpu.VMEM((3, 8, 8, W, C), BF)]
    return call(
        pre_kernel, "forward_all", 2 * 768 * ROWS * C, shape, scratch, flags, *field, own, other
    )


def backward(flags, field, gain, pre, w1_own, w1_other, w2_own, w2_other):
    weight = pltpu.VMEM((ROWS, HALF), BF)
    kept = pl.BlockSpec(memory_space=pl.ANY)
    return pl.pallas_call(
        backward_kernel,
        out_shape=jax.ShapeDtypeStruct((4, 2, W, C), BF),
        in_specs=[SMEM] + [VMEM] * 4 + [kept] + [VMEM] * 10,
        out_specs=VMEM,
        scratch_shapes=[
            pltpu.VMEM((3, 6, 4, W, C), BF),
            pltpu.VMEM((768, C), F32),
            pltpu.VMEM((3, 8, 8, W, C), BF),
            weight,
            weight,
            pltpu.VMEM((768, C), F32),
            pltpu.SemaphoreType.DMA,
        ],
        compiler_params=pltpu.CompilerParams(vmem_limit_bytes=32 * 1024 * 1024),
        cost_estimate=pl.CostEstimate(
            flops=2 * 1024 * ROWS * C, bytes_accessed=10 << 20, transcendentals=0
        ),
        name="backward",
    )(flags, *field, gain, pre, w1_own, w1_other, *w2_own, *w2_other)


def on_device(activations, cotangent, gain, first_weight, second_weight):
    tm, rows = lax.axis_index("tm"), lax.axis_index("rows")
    core, x = rows % 2, tm // 16
    flags = [tm, rows, core, lax.axis_size("tm") - 1, lax.axis_size("rows") - 1]
    flags = jnp.stack(flags + [x ^ mask for mask in (0, 1, 3, 2)]).astype(jnp.int32)

    pick = lax.broadcasted_iota(jnp.int32, (C, HALF), 0) == (
        2 * lax.broadcasted_iota(jnp.int32, (C, HALF), 1) + core
    )
    half1 = jnp.dot(first_weight, pick.astype(BF), preferred_element_type=F32).astype(BF)
    half2 = lax.dynamic_slice_in_dim(second_weight, core * HALF, HALF, axis=1)

    operand = jnp.broadcast_to(half1[None], (16,) + half1.shape)
    w1_block = lax.all_to_all(operand, "tm", 0, 0, axis_index_groups=YZ_GROUPS, tiled=True)
    w1_blocks = along_x(unpack(w1_block, UNPACK_COST))
    activations, cotangent, _ = lax.optimization_barrier((activations, cotangent, operand))

    nexts = shift(jnp.concatenate([activations[:2], cotangent], axis=0), "tm", -1)
    prevs = shift(activations[2:], "tm", 1)
    gain_half, gain_all = order_gains(flags, gain)
    nexts, prevs = lax.optimization_barrier((nexts, prevs, gain_half))[:2]
    mid = jnp.concatenate([prevs, activations, nexts[:2], cotangent, nexts[2:]], axis=0)
    edge = beyond_chip(mid)
    next_row = jnp.where(core == 0, edge[:, 1:], edge[:, :1])
    field = (mid, edge, swap_cores(jnp.concatenate([mid, next_row], axis=1)))

    w2_block = unpack(spread(after(half2, edge), "tm", YZ_GROUPS))

    gated = gate(after(gain_all, *w1_blocks))
    pre_half, squares, w1_own = forward_half(flags, gated, field, w1_blocks)
    squares_other = swap_cores(squares)
    squares_other, w2_block = lax.optimization_barrier((squares_other, w2_block))
    terms = local_terms(flags, pre_half, squares, squares_other, gain_half, field)

    total = lax.all_to_all(
        terms.reshape(4, 864, CH), "tm", 0, 0, axis_index_groups=X_GROUPS, tiled=True
    )
    w1_other = swap_cores(after(w1_own, terms))
    w2_blocks = along_x(after(w2_block, terms))
    pre = forward_all(flags, field, w1_own, w1_other)
    total, pre = lax.optimization_barrier((total, pre))

    total = lax.all_to_all(sum_terms(total), "tm", 0, 0, axis_index_groups=YZ_GROUPS, tiled=True)
    w2_far = [swap_cores(block) for block in w2_blocks]
    input_grad = backward(flags, field, gain_all, pre, w1_own, w1_other, w2_blocks, w2_far)
    total = spread(total.astype(F32).sum(0), "rows", ROW_GROUPS)
    total, input_grad = lax.optimization_barrier((total, input_grad))
    weight_grad = total.reshape(4, 2, 54, CH).sum(0).transpose(1, 0, 2).reshape(108, CH)
    return (input_grad, weight_grad)


def solution(mesh):
    return jax.shard_map(
        on_device,
        mesh=mesh,
        in_specs=(
            P("tm", "rows", None, None),
            P("tm", "rows", None, None),
            P(),
            P("tm", None),
            P("tm", None),
        ),
        out_specs=(P("tm", "rows", None, None), P("tm", None)),
        check_vma=False,
    )
```

```python
import jax
import jax.numpy as jnp
from jax import lax
from jax.experimental import pallas as pl
from jax.experimental.pallas import tpu as pltpu
from jax.sharding import PartitionSpec as P

CH = 128
C = 256
W = 32
HALF = 128
ROWS = 6912
EPS = 1e-06
BF = jnp.bfloat16
F32 = jnp.float32

YZ_GROUPS = [[x * 16 + k for k in range(16)] for x in range(4)]
X_GROUPS = [[k, k + 16, k + 32, k + 48] for k in range(16)]
ROW_GROUPS = [list(range(8))]
GAINS_COST = 1 << 36
UNPACK_COST = 1 << 36
GATE_COST = 1 << 36


def spread(block, axis, groups):
    count = len(groups[0])
    operand = jnp.broadcast_to(block[None], (count,) + block.shape)
    return lax.all_to_all(operand, axis, 0, 0, axis_index_groups=groups, tiled=True)


def swap_cores(block):
    return lax.ppermute(block, "rows", [(i, i ^ 1) for i in range(lax.axis_size("rows"))])


def shift(block, axis, distance):
    count = lax.axis_size(axis)
    route = [(i, i + distance) for i in range(count) if 0 <= i + distance < count]
    return lax.ppermute(block, axis, route)


def along_x(block):
    count = lax.axis_size("tm")
    routes = [[(i, i ^ (mask * 16)) for i in range(count)] for mask in (1, 3, 2)]
    return [block] + [lax.ppermute(block, "tm", route) for route in routes]


def beyond_chip(block):
    count = lax.axis_size("rows")
    route = [(i - 1, i) for i in range(2, count, 2)] + [(i + 1, i) for i in range(1, count - 1, 2)]
    return lax.ppermute(block, "rows", route)


def after(value, *others):
    return lax.optimization_barrier((value,) + others)[0]


def fill_shifts(out, piece, frames, at):
    count, rows = piece.shape[:2]
    flat = piece.reshape(count * rows * W, piece.shape[3]).astype(F32)
    column = lax.broadcasted_iota(jnp.int32, flat.shape, 0) % W
    before = jnp.where(column == 0, 0.0, pltpu.roll(flat, 1, 0))
    behind = jnp.where(column == W - 1, 0.0, pltpu.roll(flat, flat.shape[0] - 1, 0))
    out[1, frames, pl.ds(at, rows)] = piece
    out[0, frames, pl.ds(at, rows)] = before.astype(BF).reshape(piece.shape)
    out[2, frames, pl.ds(at, rows)] = behind.astype(BF).reshape(piece.shape)


def normalize(pre, squares, gain):
    scale = lax.rsqrt(squares * (1.0 / C) + EPS)
    normed = pre * scale
    gated = normed * gain
    sigma = 1.0 / (1.0 + jnp.exp(-gated))
    return scale, normed, gated, sigma


def fill_all(out, flags, field, base, count, far, channels=C):
    mid, edge, other = field
    core = flags[2]
    for f in range(0, count, 2):
        frames = slice(f, f + 2)
        source = slice(base + f, base + f + 2)
        fill_shifts(out, mid[source, :, :, :channels], frames, 3)
        fill_shifts(out, edge[source, :, :, :channels], frames, 1 + 4 * core)
        fill_shifts(out, other[source, :2, :, :channels], frames, 5 - 4 * core)
        if far:
            fill_shifts(out, other[source, 2:, :, :channels], frames, 0)
            for k in range(3):
                out[k, frames, 7:8] = out[k, frames, 0:1]


def place(flags, n):
    return pl.ds(pl.multiple_of(flags[5 + n] * 1728, 64), 1728)


def assemble_kernel(flags, a, b, c, d, out):
    for n, block in enumerate((a, b, c, d)):
        out[place(flags, n)] = block[...]


def gains_kernel(flags, gain, half, both):
    row = lax.broadcasted_iota(jnp.int32, (C, HALF), 0)
    col = lax.broadcasted_iota(jnp.int32, (C, HALF), 1)
    wide = jnp.broadcast_to(gain[...], (HALF, C)).T
    even = jnp.sum(jnp.where(row == 2 * col, wide, 0.0), axis=0, keepdims=True)
    odd = jnp.sum(jnp.where(row == 2 * col + 1, wide, 0.0), axis=0, keepdims=True)
    half[...] = jnp.where(flags[2] == 0, even, odd)
    both[...] = jnp.concatenate([even, odd], axis=1)


def unpack_kernel(block, out):
    rows = [block[n].astype(F32) for n in range(16)]
    out[...] = jnp.concatenate(rows, axis=0).astype(BF)


def sum_kernel(terms, out):
    total = terms[0].astype(F32) + terms[1].astype(F32)
    total = (total + terms[2].astype(F32)) + terms[3].astype(F32)
    for n in range(16):
        out[n] = total[n * 54 : n * 54 + 54].astype(BF)


def half_kernel(flags, gated, mid, edge, other, a, b, c, d, pre, squares, w1, xs):
    base = 2 - 2 * flags[2]
    fill_all(xs, flags, (mid, edge, other), 0, 6, True)
    assemble_kernel(flags, a, b, c, d, w1)
    for i in range(3):
        for j in range(3):
            lhs = jnp.concatenate(
                [xs[k, i : i + 4, pl.ds(base + j, 4)].reshape(512, C) for k in range(3)], axis=1
            )
            at = (i * 3 + j) * 3 * C
            part = jnp.dot(lhs, w1[at : at + 3 * C], preferred_element_type=F32)
            if i == 0 and j == 0:
                pre[...] = part
            else:
                pre[...] += part
    total = jnp.sum(pre[...] * pre[...], axis=1, keepdims=True)
    squares[...] = jnp.broadcast_to(total, (512, HALF))


def terms_kernel(flags, pre, own, others, gain, mid, edge, other, out, cs):
    base = 2 - 2 * flags[2]
    fill_all(cs, flags, (mid, edge, other), 8, 6, True, CH)
    _, _, gated, sigma = normalize(pre[...], own[...] + others[...], gain[...])
    act = (gated * sigma).T.astype(BF)
    taps = [(i, j, k) for i in range(3) for j in range(3) for k in range(3)]

    def operand(i, j, k):
        return cs[2 - k, 2 - i : 6 - i, pl.ds(base + 2 - j, 4)].reshape(512, CH)

    for n in range(0, 27, 2):
        pair = taps[n : n + 2]
        rhs = jnp.concatenate([operand(*tap) for tap in pair], axis=1)
        term = jnp.dot(act, rhs, preferred_element_type=F32).astype(BF)
        for m in range(len(pair)):
            out[(n + m) * HALF : (n + m + 1) * HALF] = term[:, m * CH : (m + 1) * CH]


def halves_in_order(flags, value):
    turned = jnp.concatenate([value[..., HALF:], value[..., :HALF]], axis=-1)
    return jnp.where(flags[2] == 1, turned, value)


def pre_kernel(flags, mid, edge, others, own, other, pre, acc, xs):
    fill_all(xs, flags, (mid, edge, others), 0, 8, False)
    for i in range(3):
        for j in range(3):
            lhs = jnp.concatenate(
                [xs[k, i : i + 6, j + 1 : j + 5].reshape(768, C) for k in range(3)], axis=1
            )
            at = (i * 3 + j) * 3 * C
            rhs = jnp.concatenate([own[at : at + 3 * C], other[at : at + 3 * C]], axis=1)
            part = jnp.dot(lhs, rhs, preferred_element_type=F32)
            if i == 0 and j == 0:
                acc[...] = part
            else:
                acc[...] += part
    pre[...] = halves_in_order(flags, acc[...])


def backward_kernel(
    flags, mid, edge, other, gain, pre_in, w1_own, w1_other, a, b, c, d, far_a, far_b, far_c, far_d,
    out, ps, acc, cs, w2_own, w2_other, pre, sem,
):
    copy = pltpu.make_async_copy(pre_in, pre, sem)
    copy.start()
    fill_all(cs, flags, (mid, edge, other), 8, 8, False)
    assemble_kernel(flags, a, b, c, d, w2_own)
    assemble_kernel(flags, far_a, far_b, far_c, far_d, w2_other)
    nt = (((1,), (1,)), ((), ()))
    taps = [(i, j, k) for i in range(3) for j in range(3) for k in range(3)]
    for n, (i, j, k) in enumerate(taps):
        lhs = halves_in_order(flags, cs[2 - k, 2 - i : 8 - i, 3 - j : 7 - j].reshape(768, C))
        at = n * C
        rhs = jnp.concatenate([w2_own[at : at + C], w2_other[at : at + C]], axis=1)
        part = lax.dot_general(lhs, rhs, nt, preferred_element_type=F32)
        if n == 0:
            acc[...] = part
        else:
            acc[...] += part
    copy.wait()
    row = lax.broadcasted_iota(jnp.int32, (C, C), 0)
    col = lax.broadcasted_iota(jnp.int32, (C, C), 1)
    source = jnp.where(col < HALF, 2 * col, 2 * (col - HALF) + 1)
    permutation = jnp.where(row == source, 1.0, 0.0).astype(BF)
    for t in range(6):
        natural = acc[t * 128 : t * 128 + 128]
        high = natural.astype(BF)
        rest = natural - high.astype(F32)
        middle = rest.astype(BF)
        low = (rest - middle.astype(F32)).astype(BF)
        moved = [
            jnp.dot(piece, permutation, preferred_element_type=F32) for piece in (high, middle, low)
        ]
        act_grad = (moved[0] + moved[1]) + moved[2]
        here = pre[t * 128 : t * 128 + 128]
        squares = jnp.sum(here * here, axis=-1, keepdims=True)
        scale, normed, gated, sigma = normalize(here, squares, gain[...])
        norm_grad = act_grad * sigma * (1.0 + gated * (1.0 - sigma)) * gain[...]
        pre_grad = scale * (
            norm_grad - normed * jnp.mean(norm_grad * normed, axis=-1, keepdims=True)
        )
        line = lax.broadcasted_iota(jnp.int32, pre_grad.shape, 0) // W
        outside = ((line == 0) & (flags[1] == 0)) | ((line == 3) & (flags[1] == flags[4]))
        if t >= 4:
            outside = outside | (flags[0] == flags[3])
        pre_grad = jnp.where(outside, 0.0, pre_grad)
        pre_grad = halves_in_order(flags, pre_grad).astype(BF).reshape(1, 4, W, C)
        fill_shifts(ps, pre_grad, slice(t, t + 1), 0)
    for n, (i, j, k) in enumerate(taps):
        lhs = ps[2 - k, 2 - i : 6 - i, 2 - j : 4 - j].reshape(256, C)
        at = n * C
        rhs = jnp.concatenate([w1_own[at : at + C], w1_other[at : at + C]], axis=1)
        part = lax.dot_general(lhs, rhs, nt, preferred_element_type=F32)
        if n == 0:
            acc[:256] = part
        else:
            acc[:256] += part
    out[...] = acc[:256].reshape(4, 2, W, C).astype(BF)


VMEM = pl.BlockSpec(memory_space=pltpu.VMEM)
SMEM = pl.BlockSpec(memory_space=pltpu.SMEM)


def call(kernel, name, flops, out_shape, scratch, *operands):
    smem = [SMEM] if operands[0].dtype == jnp.int32 else []
    return pl.pallas_call(
        kernel,
        out_shape=out_shape,
        in_specs=smem + [VMEM] * (len(operands) - len(smem)),
        out_specs=jax.tree.map(lambda _: VMEM, out_shape),
        scratch_shapes=scratch,
        compiler_params=pltpu.CompilerParams(vmem_limit_bytes=24 * 1024 * 1024),
        cost_estimate=pl.CostEstimate(flops=flops, bytes_accessed=1 << 20, transcendentals=0),
        name=name,
    )(*operands)


def order_gains(flags, gain):
    half = jax.ShapeDtypeStruct((1, HALF), F32)
    both = jax.ShapeDtypeStruct((1, C), F32)
    return call(gains_kernel, "gains", GAINS_COST, (half, both), [], flags, gain.reshape(1, C))


def unpack(block, cost=1):
    shape = jax.ShapeDtypeStruct((1728, HALF), BF)
    return call(unpack_kernel, "unpack", cost, shape, [], block)


def gate_kernel(value, out):
    out[...] = value[...]


def gate(value):
    shape = jax.ShapeDtypeStruct(value.shape, value.dtype)
    return call(gate_kernel, "gate", GATE_COST, shape, [], value)


def sum_terms(terms):
    shape = jax.ShapeDtypeStruct((16, 54, CH), BF)
    return call(sum_kernel, "sum_terms", 1 << 20, shape, [], terms)


def forward_half(flags, gated, field, blocks):
    shape = jax.ShapeDtypeStruct((512, HALF), F32)
    weight = jax.ShapeDtypeStruct((ROWS, HALF), BF)
    scratch = [pltpu.VMEM((3, 6, 8, W, C), BF)]
    return call(
        half_kernel, "forward_half", 4 * 512 * ROWS * HALF, (shape, shape, weight), scratch,
        flags, gated, *field, *blocks,
    )


def local_terms(flags, pre, own, others, gain, field):
    shape = jax.ShapeDtypeStruct((ROWS // 2, CH), BF)
    scratch = [pltpu.VMEM((3, 6, 8, W, CH), BF)]
    return call(
        terms_kernel, "local_terms", 4 * 512 * ROWS * HALF, shape, scratch,
        flags, pre, own, others, gain, *field,
    )


def forward_all(flags, field, own, other):
    shape = jax.ShapeDtypeStruct((768, C), F32)
    scratch = [pltpu.VMEM((768, C), F32), pltpu.VMEM((3, 8, 8, W, C), BF)]
    return call(
        pre_kernel, "forward_all", 2 * 768 * ROWS * C, shape, scratch, flags, *field, own, other
    )


def backward(flags, field, gain, pre, w1_own, w1_other, w2_own, w2_other):
    weight = pltpu.VMEM((ROWS, HALF), BF)
    kept = pl.BlockSpec(memory_space=pl.ANY)
    return pl.pallas_call(
        backward_kernel,
        out_shape=jax.ShapeDtypeStruct((4, 2, W, C), BF),
        in_specs=[SMEM] + [VMEM] * 4 + [kept] + [VMEM] * 10,
        out_specs=VMEM,
        scratch_shapes=[
            pltpu.VMEM((3, 6, 4, W, C), BF),
            pltpu.VMEM((768, C), F32),
            pltpu.VMEM((3, 8, 8, W, C), BF),
            weight,
            weight,
            pltpu.VMEM((768, C), F32),
            pltpu.SemaphoreType.DMA,
        ],
        compiler_params=pltpu.CompilerParams(vmem_limit_bytes=32 * 1024 * 1024),
        cost_estimate=pl.CostEstimate(
            flops=2 * 1024 * ROWS * C, bytes_accessed=10 << 20, transcendentals=0
        ),
        name="backward",
    )(flags, *field, gain, pre, w1_own, w1_other, *w2_own, *w2_other)


def on_device(activations, cotangent, gain, first_weight, second_weight):
    tm, rows = lax.axis_index("tm"), lax.axis_index("rows")
    core, x = rows % 2, tm // 16
    flags = [tm, rows, core, lax.axis_size("tm") - 1, lax.axis_size("rows") - 1]
    flags = jnp.stack(flags + [x ^ mask for mask in (0, 1, 3, 2)]).astype(jnp.int32)

    pick = lax.broadcasted_iota(jnp.int32, (C, HALF), 0) == (
        2 * lax.broadcasted_iota(jnp.int32, (C, HALF), 1) + core
    )
    half1 = jnp.dot(first_weight, pick.astype(BF), preferred_element_type=F32).astype(BF)
    half2 = lax.dynamic_slice_in_dim(second_weight, core * HALF, HALF, axis=1)

    operand = jnp.broadcast_to(half1[None], (16,) + half1.shape)
    w1_block = lax.all_to_all(operand, "tm", 0, 0, axis_index_groups=YZ_GROUPS, tiled=True)
    w1_blocks = along_x(unpack(w1_block, UNPACK_COST))
    activations, cotangent, _ = lax.optimization_barrier((activations, cotangent, operand))

    nexts = shift(jnp.concatenate([activations[:2], cotangent], axis=0), "tm", -1)
    prevs = shift(activations[2:], "tm", 1)
    gain_half, gain_all = order_gains(flags, gain)
    nexts, prevs = lax.optimization_barrier((nexts, prevs, gain_half))[:2]
    mid = jnp.concatenate([prevs, activations, nexts[:2], cotangent, nexts[2:]], axis=0)
    edge = beyond_chip(mid)
    next_row = jnp.where(core == 0, edge[:, 1:], edge[:, :1])
    field = (mid, edge, swap_cores(jnp.concatenate([mid, next_row], axis=1)))

    w2_block = unpack(spread(after(half2, mid, w1_blocks[0]), "tm", YZ_GROUPS))

    gated = gate(after(gain_all, w2_block, *w1_blocks))
    pre_half, squares, w1_own = forward_half(flags, gated, field, w1_blocks)
    squares_other = swap_cores(squares)
    terms = local_terms(flags, pre_half, squares, squares_other, gain_half, field)

    total = lax.all_to_all(
        terms.reshape(4, 864, CH), "tm", 0, 0, axis_index_groups=X_GROUPS, tiled=True
    )
    w1_other = swap_cores(after(w1_own, squares))
    w2_blocks = along_x(after(w2_block, terms))
    pre = forward_all(flags, field, w1_own, w1_other)
    total, pre = lax.optimization_barrier((total, pre))

    total = lax.all_to_all(sum_terms(total), "tm", 0, 0, axis_index_groups=YZ_GROUPS, tiled=True)
    w2_far = [swap_cores(block) for block in w2_blocks]
    input_grad = backward(flags, field, gain_all, pre, w1_own, w1_other, w2_blocks, w2_far)
    total = spread(total.astype(F32).sum(0), "rows", ROW_GROUPS)
    total, input_grad = lax.optimization_barrier((total, input_grad))
    weight_grad = total.reshape(4, 2, 54, CH).sum(0).transpose(1, 0, 2).reshape(108, CH)
    return (input_grad, weight_grad)


def solution(mesh):
    return jax.shard_map(
        on_device,
        mesh=mesh,
        in_specs=(
            P("tm", "rows", None, None),
            P("tm", "rows", None, None),
            P(),
            P("tm", None),
            P("tm", None),
        ),
        out_specs=(P("tm", "rows", None, None), P("tm", None)),
        check_vma=False,
    )
```

```python
import jax
import jax.numpy as jnp
from jax import lax
from jax.experimental import pallas as pl
from jax.experimental.pallas import tpu as pltpu
from jax.sharding import PartitionSpec as P

CH = 128
C = 256
W = 32
HALF = 128
ROWS = 6912
EPS = 1e-06
BF = jnp.bfloat16
F32 = jnp.float32

YZ_GROUPS = [[x * 16 + k for k in range(16)] for x in range(4)]
X_GROUPS = [[k, k + 16, k + 32, k + 48] for k in range(16)]
ROW_GROUPS = [list(range(8))]
GAINS_COST = 1 << 36
UNPACK_COST = 1 << 36
GATE_COST = 1 << 36


def spread(block, axis, groups):
    count = len(groups[0])
    operand = jnp.broadcast_to(block[None], (count,) + block.shape)
    return lax.all_to_all(operand, axis, 0, 0, axis_index_groups=groups, tiled=True)


def swap_cores(block):
    return lax.ppermute(block, "rows", [(i, i ^ 1) for i in range(lax.axis_size("rows"))])


def shift(block, axis, distance):
    count = lax.axis_size(axis)
    route = [(i, i + distance) for i in range(count) if 0 <= i + distance < count]
    return lax.ppermute(block, axis, route)


def along_x(block):
    count = lax.axis_size("tm")
    routes = [[(i, i ^ (mask * 16)) for i in range(count)] for mask in (1, 3, 2)]
    return [block] + [lax.ppermute(block, "tm", route) for route in routes]


def beyond_chip(block):
    count = lax.axis_size("rows")
    route = [(i - 1, i) for i in range(2, count, 2)] + [(i + 1, i) for i in range(1, count - 1, 2)]
    return lax.ppermute(block, "rows", route)


def after(value, *others):
    return lax.optimization_barrier((value,) + others)[0]


def fill_shifts(out, piece, frames, at):
    count, rows = piece.shape[:2]
    flat = piece.reshape(count * rows * W, piece.shape[3]).astype(F32)
    column = lax.broadcasted_iota(jnp.int32, flat.shape, 0) % W
    before = jnp.where(column == 0, 0.0, pltpu.roll(flat, 1, 0))
    behind = jnp.where(column == W - 1, 0.0, pltpu.roll(flat, flat.shape[0] - 1, 0))
    out[1, frames, pl.ds(at, rows)] = piece
    out[0, frames, pl.ds(at, rows)] = before.astype(BF).reshape(piece.shape)
    out[2, frames, pl.ds(at, rows)] = behind.astype(BF).reshape(piece.shape)


def normalize(pre, squares, gain):
    scale = lax.rsqrt(squares * (1.0 / C) + EPS)
    normed = pre * scale
    gated = normed * gain
    sigma = 1.0 / (1.0 + jnp.exp(-gated))
    return scale, normed, gated, sigma


def fill_all(out, flags, field, base, count, far, channels=C):
    mid, edge, other = field
    core = flags[2]
    for f in range(0, count, 2):
        frames = slice(f, f + 2)
        source = slice(base + f, base + f + 2)
        fill_shifts(out, mid[source, :, :, :channels], frames, 3)
        fill_shifts(out, edge[source, :, :, :channels], frames, 1 + 4 * core)
        fill_shifts(out, other[source, :2, :, :channels], frames, 5 - 4 * core)
        if far:
            fill_shifts(out, other[source, 2:, :, :channels], frames, 0)
            for k in range(3):
                out[k, frames, 7:8] = out[k, frames, 0:1]


def place(flags, n):
    return pl.ds(pl.multiple_of(flags[5 + n] * 1728, 64), 1728)


def assemble_kernel(flags, a, b, c, d, out):
    for n, block in enumerate((a, b, c, d)):
        out[place(flags, n)] = block[...]


def gains_kernel(flags, gain, half, both):
    row = lax.broadcasted_iota(jnp.int32, (C, HALF), 0)
    col = lax.broadcasted_iota(jnp.int32, (C, HALF), 1)
    wide = jnp.broadcast_to(gain[...], (HALF, C)).T
    even = jnp.sum(jnp.where(row == 2 * col, wide, 0.0), axis=0, keepdims=True)
    odd = jnp.sum(jnp.where(row == 2 * col + 1, wide, 0.0), axis=0, keepdims=True)
    half[...] = jnp.where(flags[2] == 0, even, odd)
    both[...] = jnp.concatenate([even, odd], axis=1)


def unpack_kernel(block, out):
    rows = [block[n].astype(F32) for n in range(16)]
    out[...] = jnp.concatenate(rows, axis=0).astype(BF)


def sum_kernel(terms, out):
    total = terms[0].astype(F32) + terms[1].astype(F32)
    total = (total + terms[2].astype(F32)) + terms[3].astype(F32)
    for n in range(16):
        out[n] = total[n * 54 : n * 54 + 54].astype(BF)


def half_kernel(flags, gated, mid, edge, other, a, b, c, d, pre, squares, w1, xs):
    base = 2 - 2 * flags[2]
    fill_all(xs, flags, (mid, edge, other), 0, 6, True)
    assemble_kernel(flags, a, b, c, d, w1)
    for i in range(3):
        for j in range(3):
            lhs = jnp.concatenate(
                [xs[k, i : i + 4, pl.ds(base + j, 4)].reshape(512, C) for k in range(3)], axis=1
            )
            at = (i * 3 + j) * 3 * C
            part = jnp.dot(lhs, w1[at : at + 3 * C], preferred_element_type=F32)
            if i == 0 and j == 0:
                pre[...] = part
            else:
                pre[...] += part
    total = jnp.sum(pre[...] * pre[...], axis=1, keepdims=True)
    squares[...] = jnp.broadcast_to(total, (512, HALF))


def terms_kernel(flags, pre, own, others, gain, mid, edge, other, out, cs):
    base = 2 - 2 * flags[2]
    fill_all(cs, flags, (mid, edge, other), 8, 6, True, CH)
    _, _, gated, sigma = normalize(pre[...], own[...] + others[...], gain[...])
    act = (gated * sigma).T.astype(BF)
    taps = [(i, j, k) for i in range(3) for j in range(3) for k in range(3)]

    def operand(i, j, k):
        return cs[2 - k, 2 - i : 6 - i, pl.ds(base + 2 - j, 4)].reshape(512, CH)

    for n in range(0, 27, 2):
        pair = taps[n : n + 2]
        rhs = jnp.concatenate([operand(*tap) for tap in pair], axis=1)
        term = jnp.dot(act, rhs, preferred_element_type=F32).astype(BF)
        for m in range(len(pair)):
            out[(n + m) * HALF : (n + m + 1) * HALF] = term[:, m * CH : (m + 1) * CH]


def halves_in_order(flags, value):
    turned = jnp.concatenate([value[..., HALF:], value[..., :HALF]], axis=-1)
    return jnp.where(flags[2] == 1, turned, value)


def pre_kernel(flags, mid, edge, others, own, other, pre, acc, xs):
    fill_all(xs, flags, (mid, edge, others), 0, 8, False)
    for i in range(3):
        for j in range(3):
            lhs = jnp.concatenate(
                [xs[k, i : i + 6, j + 1 : j + 5].reshape(768, C) for k in range(3)], axis=1
            )
            at = (i * 3 + j) * 3 * C
            rhs = jnp.concatenate([own[at : at + 3 * C], other[at : at + 3 * C]], axis=1)
            part = jnp.dot(lhs, rhs, preferred_element_type=F32)
            if i == 0 and j == 0:
                acc[...] = part
            else:
                acc[...] += part
    pre[...] = halves_in_order(flags, acc[...])


def backward_kernel(
    flags, mid, edge, other, gain, pre_in, w1_own, w1_other, a, b, c, d, far_a, far_b, far_c, far_d,
    out, ps, acc, cs, w2_own, w2_other, pre, sem,
):
    copy = pltpu.make_async_copy(pre_in, pre, sem)
    copy.start()
    fill_all(cs, flags, (mid, edge, other), 8, 8, False)
    assemble_kernel(flags, a, b, c, d, w2_own)
    assemble_kernel(flags, far_a, far_b, far_c, far_d, w2_other)
    nt = (((1,), (1,)), ((), ()))
    taps = [(i, j, k) for i in range(3) for j in range(3) for k in range(3)]
    for n, (i, j, k) in enumerate(taps):
        lhs = halves_in_order(flags, cs[2 - k, 2 - i : 8 - i, 3 - j : 7 - j].reshape(768, C))
        at = n * C
        rhs = jnp.concatenate([w2_own[at : at + C], w2_other[at : at + C]], axis=1)
        part = lax.dot_general(lhs, rhs, nt, preferred_element_type=F32)
        if n == 0:
            acc[...] = part
        else:
            acc[...] += part
    copy.wait()
    row = lax.broadcasted_iota(jnp.int32, (C, C), 0)
    col = lax.broadcasted_iota(jnp.int32, (C, C), 1)
    source = jnp.where(col < HALF, 2 * col, 2 * (col - HALF) + 1)
    permutation = jnp.where(row == source, 1.0, 0.0).astype(BF)
    for t in range(6):
        natural = acc[t * 128 : t * 128 + 128]
        high = natural.astype(BF)
        rest = natural - high.astype(F32)
        middle = rest.astype(BF)
        low = (rest - middle.astype(F32)).astype(BF)
        moved = [
            jnp.dot(piece, permutation, preferred_element_type=F32) for piece in (high, middle, low)
        ]
        act_grad = (moved[0] + moved[1]) + moved[2]
        here = pre[t * 128 : t * 128 + 128]
        squares = jnp.sum(here * here, axis=-1, keepdims=True)
        scale, normed, gated, sigma = normalize(here, squares, gain[...])
        norm_grad = act_grad * sigma * (1.0 + gated * (1.0 - sigma)) * gain[...]
        pre_grad = scale * (
            norm_grad - normed * jnp.mean(norm_grad * normed, axis=-1, keepdims=True)
        )
        line = lax.broadcasted_iota(jnp.int32, pre_grad.shape, 0) // W
        outside = ((line == 0) & (flags[1] == 0)) | ((line == 3) & (flags[1] == flags[4]))
        if t >= 4:
            outside = outside | (flags[0] == flags[3])
        pre_grad = jnp.where(outside, 0.0, pre_grad)
        pre_grad = halves_in_order(flags, pre_grad).astype(BF).reshape(1, 4, W, C)
        fill_shifts(ps, pre_grad, slice(t, t + 1), 0)
    for n, (i, j, k) in enumerate(taps):
        lhs = ps[2 - k, 2 - i : 6 - i, 2 - j : 4 - j].reshape(256, C)
        at = n * C
        rhs = jnp.concatenate([w1_own[at : at + C], w1_other[at : at + C]], axis=1)
        part = lax.dot_general(lhs, rhs, nt, preferred_element_type=F32)
        if n == 0:
            acc[:256] = part
        else:
            acc[:256] += part
    out[...] = acc[:256].reshape(4, 2, W, C).astype(BF)


VMEM = pl.BlockSpec(memory_space=pltpu.VMEM)
SMEM = pl.BlockSpec(memory_space=pltpu.SMEM)


def call(kernel, name, flops, out_shape, scratch, *operands):
    smem = [SMEM] if operands[0].dtype == jnp.int32 else []
    return pl.pallas_call(
        kernel,
        out_shape=out_shape,
        in_specs=smem + [VMEM] * (len(operands) - len(smem)),
        out_specs=jax.tree.map(lambda _: VMEM, out_shape),
        scratch_shapes=scratch,
        compiler_params=pltpu.CompilerParams(vmem_limit_bytes=24 * 1024 * 1024),
        cost_estimate=pl.CostEstimate(flops=flops, bytes_accessed=1 << 20, transcendentals=0),
        name=name,
    )(*operands)


def order_gains(flags, gain):
    half = jax.ShapeDtypeStruct((1, HALF), F32)
    both = jax.ShapeDtypeStruct((1, C), F32)
    return call(gains_kernel, "gains", GAINS_COST, (half, both), [], flags, gain.reshape(1, C))


def unpack(block, cost=1):
    shape = jax.ShapeDtypeStruct((1728, HALF), BF)
    return call(unpack_kernel, "unpack", cost, shape, [], block)


def gate_kernel(value, out):
    out[...] = value[...]


def gate(value):
    shape = jax.ShapeDtypeStruct(value.shape, value.dtype)
    return call(gate_kernel, "gate", GATE_COST, shape, [], value)


def sum_terms(terms):
    shape = jax.ShapeDtypeStruct((16, 54, CH), BF)
    return call(sum_kernel, "sum_terms", 1 << 20, shape, [], terms)


def forward_half(flags, gated, field, blocks):
    shape = jax.ShapeDtypeStruct((512, HALF), F32)
    weight = jax.ShapeDtypeStruct((ROWS, HALF), BF)
    scratch = [pltpu.VMEM((3, 6, 8, W, C), BF)]
    return call(
        half_kernel, "forward_half", 4 * 512 * ROWS * HALF, (shape, shape, weight), scratch,
        flags, gated, *field, *blocks,
    )


def local_terms(flags, pre, own, others, gain, field):
    shape = jax.ShapeDtypeStruct((ROWS // 2, CH), BF)
    scratch = [pltpu.VMEM((3, 6, 8, W, CH), BF)]
    return call(
        terms_kernel, "local_terms", 4 * 512 * ROWS * HALF, shape, scratch,
        flags, pre, own, others, gain, *field,
    )


def forward_all(flags, field, own, other):
    shape = jax.ShapeDtypeStruct((768, C), F32)
    scratch = [pltpu.VMEM((768, C), F32), pltpu.VMEM((3, 8, 8, W, C), BF)]
    return call(
        pre_kernel, "forward_all", 2 * 768 * ROWS * C, shape, scratch, flags, *field, own, other
    )


def backward(flags, field, gain, pre, w1_own, w1_other, w2_own, w2_other):
    weight = pltpu.VMEM((ROWS, HALF), BF)
    kept = pl.BlockSpec(memory_space=pl.ANY)
    return pl.pallas_call(
        backward_kernel,
        out_shape=jax.ShapeDtypeStruct((4, 2, W, C), BF),
        in_specs=[SMEM] + [VMEM] * 4 + [kept] + [VMEM] * 10,
        out_specs=VMEM,
        scratch_shapes=[
            pltpu.VMEM((3, 6, 4, W, C), BF),
            pltpu.VMEM((768, C), F32),
            pltpu.VMEM((3, 8, 8, W, C), BF),
            weight,
            weight,
            pltpu.VMEM((768, C), F32),
            pltpu.SemaphoreType.DMA,
        ],
        compiler_params=pltpu.CompilerParams(vmem_limit_bytes=32 * 1024 * 1024),
        cost_estimate=pl.CostEstimate(
            flops=2 * 1024 * ROWS * C, bytes_accessed=10 << 20, transcendentals=0
        ),
        name="backward",
    )(flags, *field, gain, pre, w1_own, w1_other, *w2_own, *w2_other)


def on_device(activations, cotangent, gain, first_weight, second_weight):
    tm, rows = lax.axis_index("tm"), lax.axis_index("rows")
    core, x = rows % 2, tm // 16
    flags = [tm, rows, core, lax.axis_size("tm") - 1, lax.axis_size("rows") - 1]
    flags = jnp.stack(flags + [x ^ mask for mask in (0, 1, 3, 2)]).astype(jnp.int32)

    pick = lax.broadcasted_iota(jnp.int32, (C, HALF), 0) == (
        2 * lax.broadcasted_iota(jnp.int32, (C, HALF), 1) + core
    )
    half1 = jnp.dot(first_weight, pick.astype(BF), preferred_element_type=F32).astype(BF)
    half2 = lax.dynamic_slice_in_dim(second_weight, core * HALF, HALF, axis=1)

    operand = jnp.broadcast_to(half1[None], (16,) + half1.shape)
    w1_block = lax.all_to_all(operand, "tm", 0, 0, axis_index_groups=YZ_GROUPS, tiled=True)
    w1_blocks = along_x(unpack(w1_block, UNPACK_COST))
    activations, cotangent, _ = lax.optimization_barrier((activations, cotangent, operand))

    nexts = shift(jnp.concatenate([activations[:2], cotangent], axis=0), "tm", -1)
    prevs = shift(activations[2:], "tm", 1)
    gain_half, gain_all = order_gains(flags, gain)
    nexts, prevs = lax.optimization_barrier((nexts, prevs, gain_half))[:2]
    mid = jnp.concatenate([prevs, activations, nexts[:2], cotangent, nexts[2:]], axis=0)
    edge = beyond_chip(mid)
    operand2 = jnp.broadcast_to(after(half2, edge)[None], (16,) + half2.shape)
    edge = after(edge, operand2)
    next_row = jnp.where(core == 0, edge[:, 1:], edge[:, :1])
    field = (mid, edge, swap_cores(jnp.concatenate([mid, next_row], axis=1)))

    w2_block = unpack(
        lax.all_to_all(operand2, "tm", 0, 0, axis_index_groups=YZ_GROUPS, tiled=True)
    )

    gated = gate(after(gain_all, *w1_blocks))
    pre_half, squares, w1_own = forward_half(flags, gated, field, w1_blocks)
    squares_other = swap_cores(squares)
    squares_other, w2_block = lax.optimization_barrier((squares_other, w2_block))
    terms = local_terms(flags, pre_half, squares, squares_other, gain_half, field)

    total = lax.all_to_all(
        terms.reshape(4, 864, CH), "tm", 0, 0, axis_index_groups=X_GROUPS, tiled=True
    )
    w1_other = swap_cores(after(w1_own, terms))
    w2_blocks = along_x(after(w2_block, terms))
    pre = forward_all(flags, field, w1_own, w1_other)
    total, pre = lax.optimization_barrier((total, pre))

    total = lax.all_to_all(sum_terms(total), "tm", 0, 0, axis_index_groups=YZ_GROUPS, tiled=True)
    w2_far = [swap_cores(block) for block in w2_blocks]
    input_grad = backward(flags, field, gain_all, pre, w1_own, w1_other, w2_blocks, w2_far)
    total = spread(total.astype(F32).sum(0), "rows", ROW_GROUPS)
    total, input_grad = lax.optimization_barrier((total, input_grad))
    weight_grad = total.reshape(4, 2, 54, CH).sum(0).transpose(1, 0, 2).reshape(108, CH)
    return (input_grad, weight_grad)


def solution(mesh):
    return jax.shard_map(
        on_device,
        mesh=mesh,
        in_specs=(
            P("tm", "rows", None, None),
            P("tm", "rows", None, None),
            P(),
            P("tm", None),
            P("tm", None),
        ),
        out_specs=(P("tm", "rows", None, None), P("tm", None)),
        check_vma=False,
    )
```
